32 devices in a mesh: grp: 4 (over y, x), blk: 8 (over z, core).
Axes of the slice: x: 2, y: 2, z: 4, core: 2. Of those that a mesh axis runs over, the one named last changes fastest.
Arguments:
- tokens: bfloat16 [2048, 4096], P(('blk', 'grp')), may hold values from -16 to 16
- w_query: bfloat16 [4096, 4096], P(None, 'grp'), may hold values from -0.09375 to 0.09375
- key_weight: bfloat16 [4096, 1024], P(None, 'grp'), may hold values from -0.09375 to 0.09375
- value_weight: bfloat16 [4096, 1024], P(None, 'grp'), may hold values from -0.09375 to 0.09375
- w_output: bfloat16 [4096, 4096], P('grp'), may hold values from -0.09375 to 0.09375
- block_mask: int32 [16, 16], P('blk'), may hold values from 0 to 1, as said below
- positions: int32 [2048], P('blk'), may hold values from 0 to 69629, as said below
Outputs:
- attended: bfloat16 [2048, 4096], P(('blk', 'grp'))
The draws below stay inside these ranges and needn't reach their ends.
Inputs may be any that keep to these rules, and one draw needn't show every extreme that they name: block_mask[i, j] is 1 exactly where |i - j| <= 1, where i < 1 or j < 1, or where j is one of 3 distinct blocks drawn for row i; so query blocks below 1 attend every key block. A sequence block is a run of 256 tokens from a multiple of 256. The drawn blocks of a row never lie in its own sequence block, in the two sequence blocks beside it (the last and the first count as beside each other) or in the first sequence block. Over the query blocks of one sequence block, other than those below 1, the live key blocks that lie outside that sequence block, are not the block just before or just after it, and are not below 1, number at most 2 in any one other sequence block. positions rise along the sequence by 1 or 2 per token; the last token's position is the most.
All inputs are finite; a program needn't handle non-finite values.
Results may differ from the reference program's by a relative error of at most 0.017.
Values may be sent and summed in bfloat16 or wider, within the bound.
No kernel may reach another device: no remote copies, remote signals or barrier semaphores. Data moves between devices by JAX's collectives and lax.ppermute only.
A program may use at most 64 MiB of HBM per device.

```python
import jax
import jax.numpy as jnp
from jax import lax

MODEL_WIDTH = 4096
QUERY_HEADS = 32
KEY_VALUE_HEADS = 8
HEAD_WIDTH = 128
MASK_BLOCK_TOKENS = 128
GLOB = 1
RAND = 3
SEQUENCE_TOKENS = 2048
MASK_BLOCK_COUNT = 16
ROWS = 256
N_GRP = 4


def draw_tokens(key, part):
    return jnp.clip(jax.random.normal(jax.random.fold_in(key, 31), (SEQUENCE_TOKENS, MODEL_WIDTH), jnp.float32), -6.0, 6.0).astype(jnp.bfloat16)


def pick_blocks(base_key, owner):
    per_device = ROWS // MASK_BLOCK_TOKENS
    owners = SEQUENCE_TOKENS // ROWS
    eligible = owners - 4
    owner_key = jax.random.fold_in(base_key, owner)
    order = jax.random.permutation(jax.random.fold_in(owner_key, 1), owners).astype(jnp.int32)
    excluded = (order == owner) | (order == (owner + 1) % owners) | (order == (owner + owners - 1) % owners) | (order == 0)
    ranking = excluded.astype(jnp.int32) * owners + jnp.arange(owners, dtype=jnp.int32)
    chosen = order[jnp.argsort(ranking)]
    offset_base = jax.random.randint(jax.random.fold_in(owner_key, 2), (owners,), 0, per_device)
    pick_ids = jnp.arange(per_device * RAND, dtype=jnp.int32)
    target = chosen[pick_ids % eligible]
    offset = (offset_base[target] + pick_ids // eligible) % per_device
    return (target * per_device + offset).reshape(per_device, RAND)


def draw_block_mask(key, part):
    count = SEQUENCE_TOKENS // MASK_BLOCK_TOKENS
    owners = SEQUENCE_TOKENS // ROWS
    row_ids = jnp.arange(count)[:, None]
    col_ids = jnp.arange(count)[None, :]
    band = jnp.abs(row_ids - col_ids) <= 1
    global_part = (row_ids < GLOB) | (col_ids < GLOB)
    base_key = jax.random.fold_in(key, 11)
    picks = jax.vmap(lambda owner: pick_blocks(base_key, owner))(jnp.arange(owners, dtype=jnp.int32)).reshape(count, RAND)
    random_part = jnp.any(picks[:, :, None] == jnp.arange(count)[None, None, :], axis=1)
    return (band | global_part | random_part).astype(jnp.int32)


def draw_positions(key, part):
    second_key = jax.random.fold_in(key, 22)
    steps_drawn = jax.random.randint(second_key, (SEQUENCE_TOKENS,), 1, 3).astype(jnp.int32)
    last_position = 65535 + 2 * (SEQUENCE_TOKENS - 1)
    after = jnp.cumsum(steps_drawn[::-1])[::-1] - steps_drawn
    return (last_position - after).astype(jnp.int32)


def levels(own_key, dims, pieces, low, top_value):
    factor_of, own = 1.0, jax.random.fold_in(own_key, 6)
    for axis_at, shards_of in pieces:
        heights = jnp.exp(jax.random.uniform(jax.random.fold_in(own, axis_at), (shards_of,), jnp.float32, low / len(pieces), top_value / len(pieces)))
        factor_of = factor_of * jnp.repeat(heights, dims[axis_at] // shards_of).reshape([-1 if axis == axis_at else 1 for axis in range(len(dims))])
    return factor_of


def scatter_about(own_key, dims, scale, reach, split=(), kind=jnp.bfloat16):
    level = levels(own_key, dims, split, -0.22, 0.18) if split else 1.0
    drawn = jax.random.normal(own_key, dims, jnp.float32) * scale * level
    return jnp.minimum(jnp.maximum(drawn, -reach), reach).astype(kind)


def setup_inputs(seed: int = 0) -> dict:
    splits = jax.random.split(jax.random.key(seed), 8)
    return {
        "tokens": draw_tokens(jax.random.fold_in(splits[7], 71), 0),
        "w_query": scatter_about(splits[1], (MODEL_WIDTH, QUERY_HEADS * HEAD_WIDTH), MODEL_WIDTH ** -0.5, 0.09375, ((1, 4),)),
        "key_weight": scatter_about(splits[2], (MODEL_WIDTH, KEY_VALUE_HEADS * HEAD_WIDTH), MODEL_WIDTH ** -0.5, 0.09375, ((1, 4),)),
        "value_weight": scatter_about(splits[3], (MODEL_WIDTH, KEY_VALUE_HEADS * HEAD_WIDTH), MODEL_WIDTH ** -0.5, 0.09375, ((1, 4),)),
        "w_output": scatter_about(splits[4], (QUERY_HEADS * HEAD_WIDTH, MODEL_WIDTH), (QUERY_HEADS * HEAD_WIDTH) ** -0.5, 0.09375, ((0, 4),)),
        "block_mask": draw_block_mask(jax.random.fold_in(splits[7], 71), 0),
        "positions": draw_positions(jax.random.fold_in(splits[7], 71), 0),
    }


NEG_FILL = -1e30


def rotary_position(projected, positions, heads):
    half = HEAD_WIDTH // 2
    inverse = jnp.power(jnp.float32(500000.0), -(2.0 * jnp.arange(half, dtype=jnp.float32)) / HEAD_WIDTH)
    angles = positions.astype(jnp.float32)[:, None] * inverse[None, :]
    cosine = jnp.cos(angles)[:, None, :]
    sine = jnp.sin(angles)[:, None, :]
    shaped = projected.reshape(projected.shape[0], heads, HEAD_WIDTH)
    first = shaped[..., :half]
    second = shaped[..., half:]
    turned = jnp.concatenate([first * cosine - second * sine, second * cosine + first * sine], axis=-1)
    return turned.reshape(projected.shape[0], heads * HEAD_WIDTH)


def reference(tokens, w_query, key_weight, value_weight, w_output, block_mask, positions):
    query_rows = rotary_position(jnp.dot(tokens, w_query, preferred_element_type=jnp.float32), positions, QUERY_HEADS).astype(jnp.bfloat16)
    key_rows = rotary_position(jnp.dot(tokens, key_weight, preferred_element_type=jnp.float32), positions, KEY_VALUE_HEADS).astype(jnp.bfloat16)
    value_rows = jnp.dot(tokens, value_weight, preferred_element_type=jnp.float32).astype(jnp.bfloat16)
    head_repeat_count = QUERY_HEADS // KEY_VALUE_HEADS
    scale = HEAD_WIDTH ** -0.5
    key_single_precision = key_rows.astype(jnp.float32).reshape(SEQUENCE_TOKENS, KEY_VALUE_HEADS, HEAD_WIDTH)
    value_single_precision = value_rows.astype(jnp.float32).reshape(SEQUENCE_TOKENS, KEY_VALUE_HEADS, HEAD_WIDTH)
    query_block_rows = query_rows.reshape(MASK_BLOCK_COUNT, MASK_BLOCK_TOKENS, KEY_VALUE_HEADS, head_repeat_count, HEAD_WIDTH)

    def one_block(item):
        block_query, row_mask = item
        scores = jnp.einsum('qcrd,kcd->crqk', block_query.astype(jnp.float32), key_single_precision) * scale
        live = jnp.repeat(row_mask != 0, MASK_BLOCK_TOKENS)[None, None, None, :]
        scores = jnp.where(live, scores, NEG_FILL)
        top = jnp.max(scores, axis=-1, keepdims=True)
        weights = jnp.where(live, jnp.exp(scores - top), 0.0)
        total = jnp.sum(weights, axis=-1)
        rounded = lax.optimization_barrier(weights.astype(jnp.bfloat16)).astype(jnp.float32)
        mixed = jnp.einsum('crqk,kcd->crqd', rounded, value_single_precision) / total[..., None]
        return mixed.transpose(2, 0, 1, 3).reshape(MASK_BLOCK_TOKENS, QUERY_HEADS * HEAD_WIDTH).astype(jnp.bfloat16)

    mixed_all = lax.map(one_block, (query_block_rows, block_mask)).reshape(SEQUENCE_TOKENS, QUERY_HEADS * HEAD_WIDTH)
    width = QUERY_HEADS * HEAD_WIDTH // N_GRP
    result = jnp.zeros((SEQUENCE_TOKENS, MODEL_WIDTH), jnp.float32)
    for group in range(N_GRP):
        partial_sum = jnp.dot(mixed_all[:, group * width:(group + 1) * width], w_output[group * width:(group + 1) * width], preferred_element_type=jnp.float32)
        result = result + lax.optimization_barrier(partial_sum.astype(jnp.bfloat16)).astype(jnp.float32)
    return result.astype(jnp.bfloat16)
```

```python
import functools
import math

import jax
import jax.numpy as jnp
from jax import lax
from jax.experimental import pallas as pl
from jax.experimental.pallas import tpu as pltpu
from jax.sharding import PartitionSpec as P

HEAD_WIDTH = 128
MASK_BLOCK_TOKENS = 128
ROPE_BASE = 500000.0
NEG_FILL = -1e30
WIDE = 8
QUERY_FACTOR = HEAD_WIDTH**-0.5 * math.log2(math.e)
VMEM = pl.BlockSpec(memory_space=pltpu.VMEM)
SMEM = pl.BlockSpec(memory_space=pltpu.SMEM)
MIB = 1 << 20


def params(mib):
    return pltpu.CompilerParams(vmem_limit_bytes=mib * MIB)


def turn(product, cosine, sine):
    return product * cosine + pltpu.roll(product, HEAD_WIDTH // 2, 1) * sine


def key_value_kernel(tokens_ref, key_ref, value_ref, cos_ref, sin_ref, out_ref):
    width = key_ref.shape[1]
    rows = tokens_ref[...]
    keys = jnp.dot(rows, key_ref[...], preferred_element_type=jnp.float32)
    values = jnp.dot(rows, value_ref[...], preferred_element_type=jnp.float32)
    cosine, sine = cos_ref[...], sin_ref[...]
    for at in range(0, width, HEAD_WIDTH):
        head = slice(at, at + HEAD_WIDTH)
        out_ref[:, head] = turn(keys[:, head], cosine, sine).astype(out_ref.dtype)
    out_ref[:, width:] = values.astype(out_ref.dtype)


def key_value_rows(rows, key_weight, value_weight, cosine, sine):
    width = key_weight.shape[1] + value_weight.shape[1]
    return pl.pallas_call(
        key_value_kernel,
        out_shape=jax.ShapeDtypeStruct((rows.shape[0], width), jnp.bfloat16),
        in_specs=[VMEM] * 5,
        out_specs=VMEM,
        compiler_params=params(24),
        cost_estimate=pl.CostEstimate(
            flops=2 * rows.shape[0] * rows.shape[1] * width,
            bytes_accessed=2 * (rows.size + key_weight.size + value_weight.size),
            transcendentals=0,
        ),
        name="key_value_rows",
    )(rows, key_weight, value_weight, cosine, sine)


def query_kernel(*refs):
    count = len(refs) - 4
    pieces, (weight_ref, cos_ref, sin_ref, out_ref) = refs[:count], refs[count:]
    step = 2 * HEAD_WIDTH
    rows = jnp.concatenate([piece[...] for piece in pieces], axis=0)

    @pl.loop(0, weight_ref.shape[1] // step)
    def _(tile):
        at = pl.multiple_of(tile * step, step)
        product = jnp.dot(rows, weight_ref[:, pl.ds(at, step)], preferred_element_type=jnp.float32)
        cosine, sine = cos_ref[...] * QUERY_FACTOR, sin_ref[...] * QUERY_FACTOR
        for half in range(2):
            head = turn(product[:, half * HEAD_WIDTH : (half + 1) * HEAD_WIDTH], cosine, sine)
            out_ref[:, pl.ds(at + half * HEAD_WIDTH, HEAD_WIDTH)] = head.astype(out_ref.dtype)


def query_rows(pieces, weight, cosine, sine):
    rows = sum(piece.shape[0] for piece in pieces)
    return pl.pallas_call(
        query_kernel,
        out_shape=jax.ShapeDtypeStruct((rows, weight.shape[1]), jnp.bfloat16),
        in_specs=[VMEM] * (len(pieces) + 3),
        out_specs=VMEM,
        compiler_params=params(32),
        cost_estimate=pl.CostEstimate(
            flops=2 * rows * weight.size, bytes_accessed=2 * weight.size, transcendentals=0
        ),
        name="query_rows",
    )(*pieces, weight, cosine, sine)


def attend_kernel(relatives, blk_count, groups, placed, place_ref, mask_ref, query_ref, kv_ref, weight_ref, *rest):
    out_refs, (live_ref, mixed_ref) = rest[: 2 * len(relatives)], rest[2 * len(relatives) :]
    grp, chip, core = place_ref[0], place_ref[1], place_ref[2]
    piece_rows = query_ref.shape[0] // groups
    own_blocks = mask_ref.shape[0]
    chips = blk_count // 2
    kv_heads = kv_ref.shape[1] // (2 * HEAD_WIDTH)
    repeat = query_ref.shape[1] // (kv_heads * HEAD_WIDTH)
    block = MASK_BLOCK_TOKENS
    turned = (grp * own_blocks) // groups

    for at, relative in enumerate(relatives):
        query_piece = lax.bitwise_xor(grp, relative) if placed else relative
        query_block = query_piece * piece_rows // block

        def note(index, count, query_block=query_block):
            key_block = index
            if placed:
                owner_at, inner = index // own_blocks, index % own_blocks
                shift, other = owner_at // 2, owner_at % 2
                owner = lax.rem(chip - shift + chips, chips) * 2 + lax.bitwise_xor(core, other)
                key_block = owner * own_blocks + lax.bitwise_xor(inner, turned)
            live = mask_ref[query_block, key_block]
            live_ref[count] = index
            return count + live

        count = lax.fori_loop(0, blk_count * own_blocks, note, jnp.int32(0))
        for spare in range(WIDE):
            live_ref[count + spare] = 0

        for head in range(kv_heads):
            query = jnp.concatenate(
                [
                    query_ref[
                        relative * piece_rows : (relative + 1) * piece_rows,
                        (head * repeat + q) * HEAD_WIDTH : (head * repeat + q + 1) * HEAD_WIDTH,
                    ]
                    for q in range(repeat)
                ],
                axis=0,
            )

            def step(index, state, head=head, query=query, count=count):
                top_old, total_old, mix_old = state
                first = index * WIDE
                starts = [
                    pl.multiple_of(live_ref[first + wide] * block, block) for wide in range(WIDE)
                ]
                key_cols = pl.ds(head * HEAD_WIDTH, HEAD_WIDTH)
                value_cols = pl.ds((kv_heads + head) * HEAD_WIDTH, HEAD_WIDTH)
                scores = []
                for wide, start in enumerate(starts):
                    tile = lax.dot_general(
                        query,
                        kv_ref[pl.ds(start, block), key_cols],
                        (((1,), (1,)), ((), ())),
                        preferred_element_type=jnp.float32,
                    )
                    if wide:
                        tile = tile + jnp.where(first + wide < count, 0.0, NEG_FILL)
                    scores.append(tile)
                scores = jnp.concatenate(scores, axis=1)
                top = jnp.maximum(top_old, jnp.max(scores, axis=1, keepdims=True))
                weights = jnp.exp2(scores - top)
                factor = jnp.exp2(top_old - top)
                total = total_old * factor + jnp.sum(weights, axis=1, keepdims=True)
                values = jnp.concatenate(
                    [kv_ref[pl.ds(start, block), value_cols] for start in starts], axis=0
                )
                product = jnp.dot(
                    weights.astype(jnp.bfloat16), values, preferred_element_type=jnp.float32
                )
                return top, total, mix_old * factor + product

            rows = repeat * piece_rows
            _, total, mix = lax.fori_loop(
                0,
                (count + WIDE - 1) // WIDE,
                step,
                (
                    jnp.full((rows, 1), NEG_FILL, jnp.float32),
                    jnp.zeros((rows, 1), jnp.float32),
                    jnp.zeros((rows, HEAD_WIDTH), jnp.float32),
                ),
            )
            mixed = (mix / total).astype(jnp.bfloat16)
            for q in range(repeat):
                mixed_ref[
                    at * piece_rows : (at + 1) * piece_rows,
                    (head * repeat + q) * HEAD_WIDTH : (head * repeat + q + 1) * HEAD_WIDTH,
                ] = mixed[q * piece_rows : (q + 1) * piece_rows]

    tile_cols = 512
    for side in range(2):
        side_cols = out_refs[side].shape[1]

        @pl.loop(0, side_cols // tile_cols)
        def _(tile, side=side, side_cols=side_cols):
            here = pl.multiple_of(tile * tile_cols, tile_cols)
            term = jnp.dot(
                mixed_ref[...],
                weight_ref[:, pl.ds(side * side_cols + here, tile_cols)],
                preferred_element_type=jnp.float32,
            ).astype(jnp.bfloat16)
            for at in range(len(relatives)):
                out_refs[2 * at + side][:, pl.ds(here, tile_cols)] = term[
                    at * piece_rows : (at + 1) * piece_rows
                ]


def attend(relatives, blk_count, groups, placed, place, mask, query, kv, weight):
    piece_rows = query.shape[0] // groups
    side = jax.ShapeDtypeStruct((piece_rows, weight.shape[1] // 2), jnp.bfloat16)
    return pl.pallas_call(
        functools.partial(attend_kernel, relatives, blk_count, groups, placed),
        out_shape=[side] * (2 * len(relatives)),
        in_specs=[SMEM, SMEM, VMEM, VMEM, VMEM],
        out_specs=[VMEM] * (2 * len(relatives)),
        scratch_shapes=[
            pltpu.SMEM((mask.shape[1] + 2 * WIDE,), jnp.int32),
            pltpu.VMEM((len(relatives) * piece_rows, weight.shape[0]), jnp.bfloat16),
        ],
        compiler_params=params(48),
        cost_estimate=pl.CostEstimate(
            flops=2 * len(relatives) * piece_rows * weight.size * 2,
            bytes_accessed=2 * weight.size,
            transcendentals=0,
        ),
        name="attend_project",
    )(place, mask, query, kv, weight)


def rotary_tables(rows):
    inverse = jnp.power(
        jnp.float32(ROPE_BASE),
        -(2.0 * jnp.arange(HEAD_WIDTH // 2, dtype=jnp.float32)) / HEAD_WIDTH,
    )
    angles = rows.astype(jnp.float32)[:, None] * inverse[None, :]
    cosine, sine = jnp.cos(angles), jnp.sin(angles)
    return jnp.concatenate([cosine, cosine], axis=1), jnp.concatenate([-sine, sine], axis=1)


def add(*values):
    total = values[0].astype(jnp.float32)
    for value in values[1:]:
        total = total + value.astype(jnp.float32)
    return total.astype(jnp.bfloat16)


def general_body(
    blk_count, groups, tokens, w_query, key_weight, value_weight, w_output, block_mask, positions
):
    rows = lax.all_gather(tokens, "grp", axis=0, tiled=True)
    cosine, sine = rotary_tables(positions)
    own = key_value_rows(rows, key_weight, value_weight, cosine, sine)
    kv = lax.all_gather(own, "blk", axis=0, tiled=True)
    query = query_rows((rows,), w_query, cosine, sine)
    place = jnp.zeros((3,), jnp.int32)
    order = tuple(range(groups))
    sides = attend(order, blk_count, groups, False, place, block_mask, query, kv, w_output)
    term = jnp.concatenate(
        [jnp.concatenate(sides[side::2], axis=0) for side in range(2)], axis=1
    )
    return lax.psum_scatter(term, "grp", scatter_dimension=0, tiled=True)


def square_body(
    blk_count, tokens, w_query, key_weight, value_weight, w_output, block_mask, positions
):
    grp, blk = lax.axis_index("grp"), lax.axis_index("blk")
    along_x = [(g, g ^ 1) for g in range(4)]
    along_y = [(g, g ^ 2) for g in range(4)]
    cores = [(b, b ^ 1) for b in range(blk_count)]
    chips = blk_count // 2
    piece_rows = tokens.shape[0]
    half = piece_rows // 2

    def send_x(value):
        return lax.ppermute(value, "grp", along_x)

    def send_y(value):
        return lax.ppermute(value, "grp", along_y)

    from_x, from_y = send_x(tokens), send_y(tokens)
    across = jnp.concatenate([send_y(from_x[:half]), send_x(from_y[half:])], axis=0)

    rows = positions.reshape(2, 2, piece_rows)
    rows = jnp.where(grp % 2 == 1, rows[:, ::-1], rows)
    rows = jnp.where(grp // 2 == 1, rows[::-1], rows).reshape(4 * piece_rows)
    cosine, sine = rotary_tables(rows)

    pieces = (tokens, from_x, from_y, across)
    received = []
    for relative, piece in enumerate(pieces):
        here = slice(relative * piece_rows, (relative + 1) * piece_rows)
        own = key_value_rows(piece, key_weight, value_weight, cosine[here], sine[here])
        shifted = [own] + [
            lax.ppermute(own, "blk", [(b, (b + 2 * s) % blk_count) for b in range(blk_count)])
            for s in range(1, chips)
        ]
        shifted = jnp.stack(shifted)
        received.append(jnp.stack([shifted, lax.ppermute(shifted, "blk", cores)], axis=1))
    width = received[0].shape[-1]
    kv = jnp.stack(received, axis=2).reshape(blk_count * 4 * piece_rows, width)
    query = query_rows(pieces, w_query, cosine, sine)
    place = jnp.stack([grp, blk // 2, blk % 2]).astype(jnp.int32)

    def terms(relatives):
        return attend(relatives, blk_count, 4, True, place, block_mask, query, kv, w_output)

    across_a, across_b = terms((3,))
    second_a, second_b = send_x(across_a), send_y(across_b)
    x_a, x_b, y_a, y_b = terms((1, 2))
    from_x_a, from_y_b = send_x(x_a), send_y(y_b)
    from_y_a = send_y(add(y_a, second_a))
    from_x_b = send_x(add(x_b, second_b))
    own_a, own_b = terms((0,))
    return jnp.concatenate(
        [add(own_a, from_x_a, from_y_a), add(own_b, from_y_b, from_x_b)], axis=1
    )


def solution(mesh):
    groups, blk_count = mesh.shape["grp"], mesh.shape["blk"]
    if groups == 4:
        body = functools.partial(square_body, blk_count)
    else:
        body = functools.partial(general_body, blk_count, groups)
    return jax.shard_map(
        body,
        mesh=mesh,
        in_specs=(
            P(("blk", "grp"), None),
            P(None, "grp"),
            P(None, "grp"),
            P(None, "grp"),
            P("grp", None),
            P("blk", None),
            P("blk"),
        ),
        out_specs=P(("blk", "grp"), None),
        check_vma=False,
    )
```

```python
import functools
import math

import jax
import jax.numpy as jnp
from jax import lax
from jax.experimental import pallas as pl
from jax.experimental.pallas import tpu as pltpu
from jax.sharding import PartitionSpec as P

HEAD_WIDTH = 128
MASK_BLOCK_TOKENS = 128
ROPE_BASE = 500000.0
NEG_FILL = -1e30
WIDE = 8
QUERY_FACTOR = HEAD_WIDTH**-0.5 * math.log2(math.e)
ANY = pl.BlockSpec(memory_space=pl.ANY)
VMEM = pl.BlockSpec(memory_space=pltpu.VMEM)
SMEM = pl.BlockSpec(memory_space=pltpu.SMEM)
MIB = 1 << 20


def params(mib):
    return pltpu.CompilerParams(vmem_limit_bytes=mib * MIB)


def turn(product, cosine, sine):
    return product * cosine + pltpu.roll(product, HEAD_WIDTH // 2, 1) * sine


def preload_kernel(count, *refs):
    sources, targets, sems = refs[:count], refs[-1 - count : -1], refs[-1]
    copies = [
        pltpu.make_async_copy(source, target, sems.at[at])
        for at, (source, target) in enumerate(zip(sources, targets))
    ]
    for copy in copies:
        copy.start()
    for copy in copies:
        copy.wait()


def preload(weights, after):
    return pl.pallas_call(
        functools.partial(preload_kernel, len(weights)),
        out_shape=[pltpu.VMEM(weight.shape, weight.dtype) for weight in weights],
        in_specs=[ANY] * (len(weights) + len(after)),
        out_specs=[VMEM] * len(weights),
        scratch_shapes=[pltpu.SemaphoreType.DMA((len(weights),))],
        compiler_params=params(1),
        name="preload",
    )(*[pltpu.with_memory_space_constraint(weight, pltpu.HBM) for weight in weights], *after)


def kept(weight):
    return pltpu.with_memory_space_constraint(weight, pltpu.VMEM)


def table_rows(ref, relatives, piece_rows):
    if relatives is None:
        return ref[...]
    grp = lax.axis_index("grp")
    return jnp.concatenate(
        [
            ref[pl.ds(pl.multiple_of((grp ^ r) * piece_rows, piece_rows), piece_rows)]
            for r in relatives
        ],
        axis=0,
    )


def key_value_kernel(count, relatives, *refs):
    pieces, (key_ref, value_ref, cos_ref, sin_ref, *_, out_ref) = refs[:count], refs[count:]
    width = key_ref.shape[1]
    rows = jnp.concatenate([piece[...] for piece in pieces], axis=0)
    keys = jnp.dot(rows, key_ref[...], preferred_element_type=jnp.float32)
    values = jnp.dot(rows, value_ref[...], preferred_element_type=jnp.float32)
    cosine = table_rows(cos_ref, relatives, pieces[0].shape[0])
    sine = table_rows(sin_ref, relatives, pieces[0].shape[0])
    for at in range(0, width, HEAD_WIDTH):
        head = slice(at, at + HEAD_WIDTH)
        out_ref[:, head] = turn(keys[:, head], cosine, sine).astype(out_ref.dtype)
    out_ref[:, width:] = values.astype(out_ref.dtype)


def key_value_rows(
    pieces, key_weight, value_weight, cosine, sine, relatives=None, after=(), weigh=1
):
    rows = sum(piece.shape[0] for piece in pieces)
    width = key_weight.shape[1] + value_weight.shape[1]
    return pl.pallas_call(
        functools.partial(key_value_kernel, len(pieces), relatives),
        out_shape=jax.ShapeDtypeStruct((rows, width), jnp.bfloat16),
        in_specs=[VMEM] * (len(pieces) + 4) + [ANY] * len(after),
        out_specs=VMEM,
        compiler_params=params(16),
        cost_estimate=pl.CostEstimate(
            flops=2 * rows * (key_weight.size + value_weight.size) * weigh,
            bytes_accessed=2 * (key_weight.size + value_weight.size),
            transcendentals=0,
        ),
        name="key_value_rows",
    )(*pieces, kept(key_weight), kept(value_weight), cosine, sine, *after)


def query_kernel(relatives, *refs):
    count = len(refs) - 4
    pieces, (weight_ref, cos_ref, sin_ref, out_ref) = refs[:count], refs[count:]
    step = 2 * HEAD_WIDTH
    rows = jnp.concatenate([piece[...] for piece in pieces], axis=0)

    @pl.loop(0, weight_ref.shape[1] // step)
    def _(tile):
        at = pl.multiple_of(tile * step, step)
        product = jnp.dot(rows, weight_ref[:, pl.ds(at, step)], preferred_element_type=jnp.float32)
        cosine = table_rows(cos_ref, relatives, pieces[0].shape[0]) * QUERY_FACTOR
        sine = table_rows(sin_ref, relatives, pieces[0].shape[0]) * QUERY_FACTOR
        for half in range(2):
            head = turn(product[:, half * HEAD_WIDTH : (half + 1) * HEAD_WIDTH], cosine, sine)
            out_ref[:, pl.ds(at + half * HEAD_WIDTH, HEAD_WIDTH)] = head.astype(out_ref.dtype)


def query_rows(pieces, weight, cosine, sine, relatives=None):
    rows = sum(piece.shape[0] for piece in pieces)
    return pl.pallas_call(
        functools.partial(query_kernel, relatives),
        out_shape=jax.ShapeDtypeStruct((rows, weight.shape[1]), jnp.bfloat16),
        in_specs=[VMEM] * (len(pieces) + 3),
        out_specs=VMEM,
        compiler_params=params(18),
        cost_estimate=pl.CostEstimate(
            flops=2 * rows * weight.size, bytes_accessed=2 * weight.size, transcendentals=0
        ),
        name="query_rows",
    )(*pieces, kept(weight), cosine, sine)


def attend_kernel(relatives, blk_count, groups, placed, mask_ref, query_ref, kv_ref, weight_ref, *rest):
    out_refs, (live_ref, mixed_ref) = rest[: 2 * len(relatives)], rest[2 * len(relatives) :]
    grp, blk = lax.axis_index("grp"), lax.axis_index("blk")
    chip, core = blk // 2, blk % 2
    piece_rows = query_ref.shape[0] // groups
    own_blocks = mask_ref.shape[0]
    kv_heads = kv_ref.shape[1] // (2 * HEAD_WIDTH)
    repeat = query_ref.shape[1] // (kv_heads * HEAD_WIDTH)
    block = MASK_BLOCK_TOKENS
    turned = (grp * own_blocks) // groups

    for at, relative in enumerate(relatives):
        query_piece = lax.bitwise_xor(grp, relative) if placed else relative
        query_block = query_piece * piece_rows // block

        def note(index, count, query_block=query_block):
            key_block = index
            if placed:
                owner_at, inner = index // own_blocks, index % own_blocks
                shift, other = owner_at // 2, owner_at % 2
                owner = lax.bitwise_xor(chip, shift) * 2 + lax.bitwise_xor(core, other)
                key_block = owner * own_blocks + lax.bitwise_xor(inner, turned)
            live = mask_ref[query_block, key_block]
            live_ref[count] = index
            return count + live

        count = lax.fori_loop(0, blk_count * own_blocks, note, jnp.int32(0))
        for spare in range(WIDE):
            live_ref[count + spare] = 0

        for head in range(kv_heads):
            query = jnp.concatenate(
                [
                    query_ref[
                        relative * piece_rows : (relative + 1) * piece_rows,
                        (head * repeat + q) * HEAD_WIDTH : (head * repeat + q + 1) * HEAD_WIDTH,
                    ]
                    for q in range(repeat)
                ],
                axis=0,
            )

            def step(index, state, head=head, query=query, count=count):
                top_old, total_old, mix_old = state
                first = index * WIDE
                starts = [
                    pl.multiple_of(live_ref[first + wide] * block, block) for wide in range(WIDE)
                ]
                key_cols = pl.ds(head * HEAD_WIDTH, HEAD_WIDTH)
                value_cols = pl.ds((kv_heads + head) * HEAD_WIDTH, HEAD_WIDTH)
                scores = []
                for wide, start in enumerate(starts):
                    tile = lax.dot_general(
                        query,
                        kv_ref[pl.ds(start, block), key_cols],
                        (((1,), (1,)), ((), ())),
                        preferred_element_type=jnp.float32,
                    )
                    if wide:
                        tile = tile + jnp.where(first + wide < count, 0.0, NEG_FILL)
                    scores.append(tile)
                scores = jnp.concatenate(scores, axis=1)
                top = jnp.maximum(top_old, jnp.max(scores, axis=1, keepdims=True))
                weights = jnp.exp2(scores - top)
                factor = jnp.exp2(top_old - top)
                total = total_old * factor + jnp.sum(weights, axis=1, keepdims=True)
                values = jnp.concatenate(
                    [kv_ref[pl.ds(start, block), value_cols] for start in starts], axis=0
                )
                product = jnp.dot(
                    weights.astype(jnp.bfloat16), values, preferred_element_type=jnp.float32
                )
                return top, total, mix_old * factor + product

            rows = repeat * piece_rows
            _, total, mix = lax.fori_loop(
                0,
                (count + WIDE - 1) // WIDE,
                step,
                (
                    jnp.full((rows, 1), NEG_FILL, jnp.float32),
                    jnp.zeros((rows, 1), jnp.float32),
                    jnp.zeros((rows, HEAD_WIDTH), jnp.float32),
                ),
            )
            mixed = (mix / total).astype(jnp.bfloat16)
            for q in range(repeat):
                mixed_ref[
                    at * piece_rows : (at + 1) * piece_rows,
                    (head * repeat + q) * HEAD_WIDTH : (head * repeat + q + 1) * HEAD_WIDTH,
                ] = mixed[q * piece_rows : (q + 1) * piece_rows]

    tile_cols = 512
    for side in range(2):
        side_cols = out_refs[side].shape[1]

        @pl.loop(0, side_cols // tile_cols)
        def _(tile, side=side, side_cols=side_cols):
            here = pl.multiple_of(tile * tile_cols, tile_cols)
            term = jnp.dot(
                mixed_ref[...],
                weight_ref[:, pl.ds(side * side_cols + here, tile_cols)],
                preferred_element_type=jnp.float32,
            ).astype(jnp.bfloat16)
            for at in range(len(relatives)):
                out_refs[2 * at + side][:, pl.ds(here, tile_cols)] = term[
                    at * piece_rows : (at + 1) * piece_rows
                ]


def gather_kernel(piece_counts, *refs):
    parts, out_ref = refs[:-1], refs[-1]
    shifts = parts[0].shape[0]
    piece_rows = parts[0].shape[1] // piece_counts[0]
    total = sum(piece_counts)
    for shift in range(shifts):
        for core in range(2):
            piece = 0
            for chunk, pieces in enumerate(piece_counts):
                at = ((shift * 2 + core) * total + piece) * piece_rows
                out_ref[at : at + pieces * piece_rows] = parts[2 * chunk + core][shift]
                piece += pieces


def gather_rows(piece_counts, parts):
    shifts, _, width = parts[0].shape
    rows = sum(2 * shifts * part.shape[1] for part in parts[::2])
    return pl.pallas_call(
        functools.partial(gather_kernel, piece_counts),
        out_shape=jax.ShapeDtypeStruct((rows, width), jnp.bfloat16),
        in_specs=[VMEM] * len(parts),
        out_specs=VMEM,
        compiler_params=params(12),
        name="key_value_gather",
    )(*parts)


def attend(relatives, blk_count, groups, placed, mask, query, kv, weight):
    piece_rows = query.shape[0] // groups
    side = jax.ShapeDtypeStruct((piece_rows, weight.shape[1] // 2), jnp.bfloat16)
    return pl.pallas_call(
        functools.partial(attend_kernel, relatives, blk_count, groups, placed),
        out_shape=[side] * (2 * len(relatives)),
        in_specs=[SMEM, VMEM, VMEM, VMEM],
        out_specs=[VMEM] * (2 * len(relatives)),
        scratch_shapes=[
            pltpu.SMEM((mask.shape[1] + 2 * WIDE,), jnp.int32),
            pltpu.VMEM((len(relatives) * piece_rows, weight.shape[0]), jnp.bfloat16),
        ],
        compiler_params=params(20 if placed else 48),
        cost_estimate=pl.CostEstimate(
            flops=2 * len(relatives) * piece_rows * weight.size * 2,
            bytes_accessed=2 * weight.size,
            transcendentals=0,
        ),
        name="attend_project",
    )(mask, query, kv, kept(weight))


def rotary_tables(positions):
    half = HEAD_WIDTH // 2
    inverse = jnp.power(
        jnp.float32(ROPE_BASE),
        -(2.0 * (jnp.arange(HEAD_WIDTH) % half).astype(jnp.float32)) / HEAD_WIDTH,
    )
    sign = jnp.where(jnp.arange(HEAD_WIDTH) < half, -1.0, 1.0)
    angles = positions.astype(jnp.float32)[:, None] * inverse[None, :]
    return jnp.cos(angles), jnp.sin(angles) * sign[None, :]


def add(*values):
    total = values[0].astype(jnp.float32)
    for value in values[1:]:
        total = total + value.astype(jnp.float32)
    return total.astype(jnp.bfloat16)


def general_body(
    blk_count, groups, tokens, w_query, key_weight, value_weight, w_output, block_mask, positions
):
    rows = lax.all_gather(tokens, "grp", axis=0, tiled=True)
    cosine, sine = rotary_tables(positions)
    own = key_value_rows((rows,), key_weight, value_weight, cosine, sine)
    kv = lax.all_gather(own, "blk", axis=0, tiled=True)
    query = query_rows((rows,), w_query, cosine, sine)
    order = tuple(range(groups))
    sides = attend(order, blk_count, groups, False, block_mask, query, kv, w_output)
    term = jnp.concatenate(
        [jnp.concatenate(sides[side::2], axis=0) for side in range(2)], axis=1
    )
    return lax.psum_scatter(term, "grp", scatter_dimension=0, tiled=True)


def square_body(
    blk_count, tokens, w_query, key_weight, value_weight, w_output, block_mask, positions
):
    along_x = [(g, g ^ 1) for g in range(4)]
    along_y = [(g, g ^ 2) for g in range(4)]
    cores = [(b, b ^ 1) for b in range(blk_count)]
    chips = blk_count // 2
    piece_rows = tokens.shape[0]
    half = piece_rows // 2

    def send_x(value):
        return lax.ppermute(value, "grp", along_x)

    def send_y(value):
        return lax.ppermute(value, "grp", along_y)

    from_x, from_y = send_x(tokens), send_y(tokens)
    across = jnp.concatenate([send_y(from_x[:half]), send_x(from_y[half:])], axis=0)

    cosine, sine = rotary_tables(positions)
    key_weight, value_weight, w_query, w_output = preload(
        (key_weight, value_weight, w_query, w_output), (cosine, sine)
    )

    def exchange(pieces, first, after, weigh):
        relatives = tuple(range(first, first + len(pieces)))
        own = key_value_rows(
            pieces, key_weight, value_weight, cosine, sine, relatives, after, weigh
        )
        shifted = [own] + [
            lax.ppermute(own, "blk", [(b, b ^ (2 * s)) for b in range(blk_count)])
            for s in range(1, chips)
        ]
        shifted = jnp.stack(shifted)
        return [shifted, lax.ppermute(shifted, "blk", cores)]

    pieces = (tokens, from_x, from_y, across)
    chunks = ((tokens,), (from_x, from_y), (across,))
    parts, first = [], 0
    for chunk in chunks:
        parts += exchange(chunk, first, parts[:2], 40 if len(chunk) > 1 else 1)
        first += len(chunk)
    kv = gather_rows(tuple(len(chunk) for chunk in chunks), parts)
    query = query_rows(pieces, w_query, cosine, sine, tuple(range(4)))

    def terms(relatives):
        return attend(relatives, blk_count, 4, True, block_mask, query, kv, w_output)

    across_a, across_b = terms((3,))
    second_a, second_b = send_x(across_a), send_y(across_b)
    x_a, x_b, y_a, y_b = terms((1, 2))
    from_x_a, from_y_b = send_x(x_a), send_y(y_b)
    from_y_a = send_y(add(y_a, second_a))
    from_x_b = send_x(add(x_b, second_b))
    own_a, own_b = terms((0,))
    return jnp.concatenate(
        [add(own_a, from_x_a, from_y_a), add(own_b, from_y_b, from_x_b)], axis=1
    )


def solution(mesh):
    groups, blk_count = mesh.shape["grp"], mesh.shape["blk"]
    if groups == 4 and blk_count & (blk_count - 1) == 0:
        body = functools.partial(square_body, blk_count)
    else:
        body = functools.partial(general_body, blk_count, groups)
    return jax.shard_map(
        body,
        mesh=mesh,
        in_specs=(
            P(("blk", "grp"), None),
            P(None, "grp"),
            P(None, "grp"),
            P(None, "grp"),
            P("grp", None),
            P("blk", None),
            P("blk"),
        ),
        out_specs=P(("blk", "grp"), None),
        check_vma=False,
    )
```

```python
import functools
import math

import jax
import jax.numpy as jnp
from jax import lax
from jax.experimental import pallas as pl
from jax.experimental.pallas import tpu as pltpu
from jax.sharding import PartitionSpec as P

HEAD_WIDTH = 128
MASK_BLOCK_TOKENS = 128
ROPE_BASE = 500000.0
NEG_FILL = -1e30
WIDE = 8
QUERY_FACTOR = HEAD_WIDTH**-0.5 * math.log2(math.e)
ANY = pl.BlockSpec(memory_space=pl.ANY)
VMEM = pl.BlockSpec(memory_space=pltpu.VMEM)
SMEM = pl.BlockSpec(memory_space=pltpu.SMEM)
MIB = 1 << 20


def params(mib):
    return pltpu.CompilerParams(vmem_limit_bytes=mib * MIB)


def turn(product, cosine, sine):
    return product * cosine + pltpu.roll(product, HEAD_WIDTH // 2, 1) * sine


def preload_kernel(count, *refs):
    sources, targets, sems = refs[:count], refs[-1 - count : -1], refs[-1]
    copies = [
        pltpu.make_async_copy(source, target, sems.at[at])
        for at, (source, target) in enumerate(zip(sources, targets))
    ]
    for copy in copies:
        copy.start()
    for copy in copies:
        copy.wait()


def preload(weights, after):
    return pl.pallas_call(
        functools.partial(preload_kernel, len(weights)),
        out_shape=[pltpu.VMEM(weight.shape, weight.dtype) for weight in weights],
        in_specs=[ANY] * (len(weights) + len(after)),
        out_specs=[VMEM] * len(weights),
        scratch_shapes=[pltpu.SemaphoreType.DMA((len(weights),))],
        compiler_params=params(1),
        name="preload",
    )(*[pltpu.with_memory_space_constraint(weight, pltpu.HBM) for weight in weights], *after)


def kept(weight):
    return pltpu.with_memory_space_constraint(weight, pltpu.VMEM)


def group_of(slot, core):
    return {0: 0, 1: 1 + core, 2: 2 - core, 3: 3}[slot]


def chip_of(at, chips):
    shift, step, place = 0, chips // 2, 1
    while step:
        shift = shift ^ ((at // place % 2) * (2 * step - 1))
        step, place = step // 2, place * 2
    return shift


def table_rows(ref, slots, piece_rows):
    if slots is None:
        return ref[...]
    grp, core = lax.axis_index("grp"), lax.axis_index("blk") % 2
    rows = []
    for slot in slots:
        at = lax.bitwise_xor(grp, group_of(slot, core)) * piece_rows
        rows.append(ref[pl.ds(pl.multiple_of(at, piece_rows), piece_rows)])
    return jnp.concatenate(rows, axis=0)


def key_value_kernel(count, slots, *refs):
    pieces, (key_ref, value_ref, cos_ref, sin_ref, *_, out_ref) = refs[:count], refs[count:]
    width = key_ref.shape[1]
    rows = jnp.concatenate([piece[...] for piece in pieces], axis=0)
    keys = jnp.dot(rows, key_ref[...], preferred_element_type=jnp.float32)
    values = jnp.dot(rows, value_ref[...], preferred_element_type=jnp.float32)
    cosine = table_rows(cos_ref, slots, pieces[0].shape[0])
    sine = table_rows(sin_ref, slots, pieces[0].shape[0])
    for at in range(0, width, HEAD_WIDTH):
        head = slice(at, at + HEAD_WIDTH)
        out_ref[:, head] = turn(keys[:, head], cosine, sine).astype(out_ref.dtype)
    out_ref[:, width:] = values.astype(out_ref.dtype)


def key_value_rows(
    pieces, key_weight, value_weight, cosine, sine, slots=None, after=(), weigh=1
):
    rows = sum(piece.shape[0] for piece in pieces)
    width = key_weight.shape[1] + value_weight.shape[1]
    return pl.pallas_call(
        functools.partial(key_value_kernel, len(pieces), slots),
        out_shape=jax.ShapeDtypeStruct((rows, width), jnp.bfloat16),
        in_specs=[VMEM] * (len(pieces) + 4) + [ANY] * len(after),
        out_specs=VMEM,
        compiler_params=params(16),
        cost_estimate=pl.CostEstimate(
            flops=2 * rows * (key_weight.size + value_weight.size) * weigh,
            bytes_accessed=2 * (key_weight.size + value_weight.size),
            transcendentals=0,
        ),
        name="key_value_rows",
    )(*pieces, key_weight, value_weight, cosine, sine, *after)


def query_kernel(slots, *refs):
    count = len(refs) - 4
    pieces, (weight_ref, cos_ref, sin_ref, out_ref) = refs[:count], refs[count:]
    step = 2 * HEAD_WIDTH
    rows = jnp.concatenate([piece[...] for piece in pieces], axis=0)

    @pl.loop(0, weight_ref.shape[1] // step)
    def _(tile):
        at = pl.multiple_of(tile * step, step)
        product = jnp.dot(rows, weight_ref[:, pl.ds(at, step)], preferred_element_type=jnp.float32)
        cosine = table_rows(cos_ref, slots, pieces[0].shape[0]) * QUERY_FACTOR
        sine = table_rows(sin_ref, slots, pieces[0].shape[0]) * QUERY_FACTOR
        for half in range(2):
            head = turn(product[:, half * HEAD_WIDTH : (half + 1) * HEAD_WIDTH], cosine, sine)
            out_ref[:, pl.ds(at + half * HEAD_WIDTH, HEAD_WIDTH)] = head.astype(out_ref.dtype)


def query_rows(pieces, weight, cosine, sine, slots=None):
    rows = sum(piece.shape[0] for piece in pieces)
    return pl.pallas_call(
        functools.partial(query_kernel, slots),
        out_shape=jax.ShapeDtypeStruct((rows, weight.shape[1]), jnp.bfloat16),
        in_specs=[VMEM] * (len(pieces) + 3),
        out_specs=VMEM,
        compiler_params=params(18),
        cost_estimate=pl.CostEstimate(
            flops=2 * rows * weight.size, bytes_accessed=2 * weight.size, transcendentals=0
        ),
        name="query_rows",
    )(*pieces, weight, cosine, sine)


def attend_kernel(slots, groups, placed, mask_ref, query_ref, kv_ref, weight_ref, *rest):
    out_refs, (live_ref, mixed_ref) = rest[: len(slots)], rest[len(slots) :]
    grp, core = lax.axis_index("grp"), lax.axis_index("blk") % 2
    piece_rows = query_ref.shape[0] // groups
    kv_heads = kv_ref.shape[1] // (2 * HEAD_WIDTH)
    repeat = query_ref.shape[1] // (kv_heads * HEAD_WIDTH)
    block = MASK_BLOCK_TOKENS

    for at, slot in enumerate(slots):
        query_piece = lax.bitwise_xor(grp, group_of(slot, core)) if placed else slot
        query_block = query_piece * piece_rows // block

        def note(index, count, query_block=query_block):
            live_ref[count] = index
            return count + mask_ref[query_block, index]

        count = lax.fori_loop(0, mask_ref.shape[1], note, jnp.int32(0))
        for spare in range(WIDE):
            live_ref[count + spare] = 0

        for head in range(kv_heads):
            query = jnp.concatenate(
                [
                    query_ref[
                        slot * piece_rows : (slot + 1) * piece_rows,
                        (head * repeat + q) * HEAD_WIDTH : (head * repeat + q + 1) * HEAD_WIDTH,
                    ]
                    for q in range(repeat)
                ],
                axis=0,
            )

            def step(index, state, head=head, query=query, count=count):
                top_old, total_old, mix_old = state
                first = index * WIDE
                starts = [
                    pl.multiple_of(live_ref[first + wide] * block, block) for wide in range(WIDE)
                ]
                key_cols = pl.ds(head * HEAD_WIDTH, HEAD_WIDTH)
                value_cols = pl.ds((kv_heads + head) * HEAD_WIDTH, HEAD_WIDTH)
                scores = []
                for wide, start in enumerate(starts):
                    tile = lax.dot_general(
                        query,
                        kv_ref[pl.ds(start, block), key_cols],
                        (((1,), (1,)), ((), ())),
                        preferred_element_type=jnp.float32,
                    )
                    if wide:
                        tile = tile + jnp.where(first + wide < count, 0.0, NEG_FILL)
                    scores.append(tile)
                scores = jnp.concatenate(scores, axis=1)
                top = jnp.maximum(top_old, jnp.max(scores, axis=1, keepdims=True))
                weights = jnp.exp2(scores - top)
                factor = jnp.exp2(top_old - top)
                total = total_old * factor + jnp.sum(weights, axis=1, keepdims=True)
                values = jnp.concatenate(
                    [kv_ref[pl.ds(start, block), value_cols] for start in starts], axis=0
                )
                product = jnp.dot(
                    weights.astype(jnp.bfloat16), values, preferred_element_type=jnp.float32
                )
                return top, total, mix_old * factor + product

            rows = repeat * piece_rows
            _, total, mix = lax.fori_loop(
                0,
                (count + WIDE - 1) // WIDE,
                step,
                (
                    jnp.full((rows, 1), NEG_FILL, jnp.float32),
                    jnp.zeros((rows, 1), jnp.float32),
                    jnp.zeros((rows, HEAD_WIDTH), jnp.float32),
                ),
            )
            mixed = (mix / total).astype(jnp.bfloat16)
            for q in range(repeat):
                mixed_ref[
                    at * piece_rows : (at + 1) * piece_rows,
                    (head * repeat + q) * HEAD_WIDTH : (head * repeat + q + 1) * HEAD_WIDTH,
                ] = mixed[q * piece_rows : (q + 1) * piece_rows]

    tile_cols = 512

    @pl.loop(0, weight_ref.shape[1] // tile_cols)
    def _(tile):
        here = pl.ds(pl.multiple_of(tile * tile_cols, tile_cols), tile_cols)
        term = jnp.dot(
            mixed_ref[...], weight_ref[:, here], preferred_element_type=jnp.float32
        ).astype(jnp.bfloat16)
        for at in range(len(slots)):
            out_refs[at][:, here] = term[at * piece_rows : (at + 1) * piece_rows]


def gather_kernel(chunks, *refs):
    parts, out_ref = refs[:-1], refs[-1]
    grp, blk = lax.axis_index("grp"), lax.axis_index("blk")

    def place(owner, group, rows):
        at = (owner * 4 + group) * rows.shape[0]
        out_ref[pl.ds(pl.multiple_of(at, rows.shape[0]), rows.shape[0])] = rows

    at = 0
    for slots in chunks:
        shifts = parts[at].shape[0]
        piece_rows = parts[at].shape[1] // len(slots)
        for other in range(2):
            core = lax.bitwise_xor(blk % 2, other)
            for shift in range(shifts):
                owner = lax.bitwise_xor(blk // 2, chip_of(shift, shifts)) * 2 + core
                for index, slot in enumerate(slots):
                    group = lax.bitwise_xor(grp, group_of(slot, core))
                    rows = slice(index * piece_rows, (index + 1) * piece_rows)
                    place(owner, group, parts[at + other][shift, rows])
        at += 2


def gather_rows(chunks, parts, rows):
    return pl.pallas_call(
        functools.partial(gather_kernel, chunks),
        out_shape=jax.ShapeDtypeStruct((rows, parts[0].shape[-1]), jnp.bfloat16),
        in_specs=[VMEM] * len(parts),
        out_specs=VMEM,
        compiler_params=params(12),
        name="key_value_gather",
    )(*parts)


def attend(slots, groups, placed, mask, query, kv, weight):
    piece_rows = query.shape[0] // groups
    term = jax.ShapeDtypeStruct((piece_rows, weight.shape[1]), jnp.bfloat16)
    return pl.pallas_call(
        functools.partial(attend_kernel, slots, groups, placed),
        out_shape=[term] * len(slots),
        in_specs=[SMEM, VMEM, VMEM, VMEM],
        out_specs=[VMEM] * len(slots),
        scratch_shapes=[
            pltpu.SMEM((mask.shape[1] + 2 * WIDE,), jnp.int32),
            pltpu.VMEM((len(slots) * piece_rows, weight.shape[0]), jnp.bfloat16),
        ],
        compiler_params=params(20 if placed else 48),
        cost_estimate=pl.CostEstimate(
            flops=2 * len(slots) * piece_rows * weight.size * 2,
            bytes_accessed=2 * weight.size,
            transcendentals=0,
        ),
        name="attend_project",
    )(mask, query, kv, weight)


def rotary_tables(positions):
    half = HEAD_WIDTH // 2
    inverse = jnp.power(
        jnp.float32(ROPE_BASE),
        -(2.0 * (jnp.arange(HEAD_WIDTH) % half).astype(jnp.float32)) / HEAD_WIDTH,
    )
    sign = jnp.where(jnp.arange(HEAD_WIDTH) < half, -1.0, 1.0)
    angles = positions.astype(jnp.float32)[:, None] * inverse[None, :]
    return jnp.cos(angles), jnp.sin(angles) * sign[None, :]


def add(*values):
    total = values[0].astype(jnp.float32)
    for value in values[1:]:
        total = total + value.astype(jnp.float32)
    return total.astype(jnp.bfloat16)


def general_body(
    blk_count, groups, tokens, w_query, key_weight, value_weight, w_output, block_mask, positions
):
    rows = lax.all_gather(tokens, "grp", axis=0, tiled=True)
    cosine, sine = rotary_tables(positions)
    own = key_value_rows((rows,), key_weight, value_weight, cosine, sine)
    kv = lax.all_gather(own, "blk", axis=0, tiled=True)
    query = query_rows((rows,), w_query, cosine, sine)
    order = tuple(range(groups))
    terms = attend(order, groups, False, block_mask, query, kv, w_output)
    term = jnp.concatenate(terms, axis=0)
    return lax.psum_scatter(term, "grp", scatter_dimension=0, tiled=True)


def square_body(
    blk_count, tokens, w_query, key_weight, value_weight, w_output, block_mask, positions
):
    chips = blk_count // 2

    def send(value, slot):
        pairs = []
        for g in range(4):
            for b in range(blk_count):
                pairs.append((g * blk_count + b, (g ^ group_of(slot, b % 2)) * blk_count + b))
        return lax.ppermute(value, ("grp", "blk"), pairs)

    first, second = send(tokens, 1), send(tokens, 2)
    across = send(first, 2)

    cosine, sine = rotary_tables(positions)
    key_weight, value_weight = preload((key_weight, value_weight), (cosine, sine))

    def exchange(slots, after=(), weigh=1, beside=None, direct=False):
        own = key_value_rows(
            [pieces[slot] for slot in slots],
            kept(key_weight),
            kept(value_weight),
            cosine,
            sine,
            slots,
            after,
            weigh,
        )
        held = own[None]
        if direct:
            sent = [
                lax.ppermute(own, "blk", [(b, b ^ (2 * chip_of(at, chips))) for b in range(blk_count)])
                for at in range(1, chips)
            ]
            held = jnp.stack([own, *sent])
        step = 0 if direct else chips // 2
        while step:
            mask = 4 * step - 2
            pairs = [(b, b ^ mask) for b in range(blk_count)]
            held = jnp.concatenate([held, lax.ppermute(held, "blk", pairs)], axis=0)
            step //= 2
        if beside is not None:
            held, beside = lax.optimization_barrier((held, beside))
        both = [held, lax.ppermute(held, "blk", [(b, b ^ 1) for b in range(blk_count)])]
        return own, both, beside

    pieces = (tokens, first, second, across)
    rows_0, parts_0, _ = exchange((0,), direct=True)
    rows_1, parts_1, _ = exchange((1,), (rows_0,), direct=True)
    query = query_rows(pieces, w_query, cosine, sine, tuple(range(4)))
    _, parts_2, query = exchange((2, 3), (*parts_0, *parts_1), beside=query, direct=True)
    chunks = ((0,), (1,), (2, 3))
    parts = parts_0 + parts_1 + parts_2
    kv = gather_rows(chunks, parts, blk_count * positions.shape[0])

    def terms(slots):
        return attend(slots, 4, True, block_mask, query, kv, w_output)

    (term_across,) = terms((3,))
    sent_across = send(term_across, 2)
    term_first, term_second = terms((1, 2))
    sent_second = send(term_second, 2)
    sent_first = send(add(term_first, sent_across), 1)
    (term_own,) = terms((0,))
    return add(term_own, sent_second, sent_first)


def solution(mesh):
    groups, blk_count = mesh.shape["grp"], mesh.shape["blk"]
    if groups == 4 and blk_count & (blk_count - 1) == 0:
        body = functools.partial(square_body, blk_count)
    else:
        body = functools.partial(general_body, blk_count, groups)
    return jax.shard_map(
        body,
        mesh=mesh,
        in_specs=(
            P(("blk", "grp"), None),
            P(None, "grp"),
            P(None, "grp"),
            P(None, "grp"),
            P("grp", None),
            P("blk", None),
            P("blk"),
        ),
        out_specs=P(("blk", "grp"), None),
        check_vma=False,
    )
```

```python
import functools
import math

import jax
import jax.numpy as jnp
from jax import lax
from jax.experimental import pallas as pl
from jax.experimental.pallas import tpu as pltpu
from jax.sharding import PartitionSpec as P

HEAD_WIDTH = 128
MASK_BLOCK_TOKENS = 128
ROPE_BASE = 500000.0
NEG_FILL = -1e30
QUERY_COLS = 1024
WIDE = 8
SURE = 6
QUERY_FACTOR = HEAD_WIDTH**-0.5 * math.log2(math.e)
ANY = pl.BlockSpec(memory_space=pl.ANY)
VMEM = pl.BlockSpec(memory_space=pltpu.VMEM)
SMEM = pl.BlockSpec(memory_space=pltpu.SMEM)
MIB = 1 << 20


def params(mib):
    return pltpu.CompilerParams(vmem_limit_bytes=mib * MIB)


def turn(product, cosine, sine):
    return product * cosine + pltpu.roll(product, HEAD_WIDTH // 2, 1) * sine


def preload_kernel(count, *refs):
    sources, targets, sems = refs[:count], refs[-1 - count : -1], refs[-1]
    copies = [
        pltpu.make_async_copy(source, target, sems.at[at])
        for at, (source, target) in enumerate(zip(sources, targets))
    ]
    for copy in copies:
        copy.start()
    for copy in copies:
        copy.wait()


def preload(weights, after):
    return pl.pallas_call(
        functools.partial(preload_kernel, len(weights)),
        out_shape=[pltpu.VMEM(weight.shape, weight.dtype) for weight in weights],
        in_specs=[ANY] * (len(weights) + len(after)),
        out_specs=[VMEM] * len(weights),
        scratch_shapes=[pltpu.SemaphoreType.DMA((len(weights),))],
        compiler_params=params(1),
        name="preload",
    )(*[pltpu.with_memory_space_constraint(weight, pltpu.HBM) for weight in weights], *after)


def kept(weight):
    return pltpu.with_memory_space_constraint(weight, pltpu.VMEM)


def group_of(slot, core):
    return {0: 0, 1: 1 + core, 2: 2 - core, 3: 3}[slot]


def chip_of(at, chips):
    shift, step, place = 0, chips // 2, 1
    while step:
        shift = shift ^ ((at // place % 2) * (2 * step - 1))
        step, place = step // 2, place * 2
    return shift


def table_rows(ref, slots, piece_rows):
    if slots is None:
        return ref[...]
    grp, core = lax.axis_index("grp"), lax.axis_index("blk") % 2
    rows = []
    for slot in slots:
        at = lax.bitwise_xor(grp, group_of(slot, core)) * piece_rows
        rows.append(ref[pl.ds(pl.multiple_of(at, piece_rows), piece_rows)])
    return jnp.concatenate(rows, axis=0)


def key_value_kernel(count, slots, *refs):
    pieces, (key_ref, value_ref, cos_ref, sin_ref, *_, out_ref) = refs[:count], refs[count:]
    width = key_ref.shape[1]
    rows = jnp.concatenate([piece[...] for piece in pieces], axis=0)
    keys = jnp.dot(rows, key_ref[...], preferred_element_type=jnp.float32)
    values = jnp.dot(rows, value_ref[...], preferred_element_type=jnp.float32)
    cosine = table_rows(cos_ref, slots, pieces[0].shape[0])
    sine = table_rows(sin_ref, slots, pieces[0].shape[0])
    for at in range(0, width, HEAD_WIDTH):
        head = slice(at, at + HEAD_WIDTH)
        out_ref[:, head] = turn(keys[:, head], cosine, sine).astype(out_ref.dtype)
    out_ref[:, width:] = values.astype(out_ref.dtype)


def key_value_rows(
    pieces, key_weight, value_weight, cosine, sine, slots=None, after=(), weigh=1
):
    rows = sum(piece.shape[0] for piece in pieces)
    width = key_weight.shape[1] + value_weight.shape[1]
    return pl.pallas_call(
        functools.partial(key_value_kernel, len(pieces), slots),
        out_shape=jax.ShapeDtypeStruct((rows, width), jnp.bfloat16),
        in_specs=[VMEM] * (len(pieces) + 4) + [ANY] * len(after),
        out_specs=VMEM,
        compiler_params=params(16),
        cost_estimate=pl.CostEstimate(
            flops=2 * rows * (key_weight.size + value_weight.size) * weigh,
            bytes_accessed=2 * (key_weight.size + value_weight.size),
            transcendentals=0,
        ),
        name="key_value_rows",
    )(*pieces, key_weight, value_weight, cosine, sine, *after)


def query_kernel(slots, *refs):
    count = len(refs) - 4
    pieces, (weight_ref, cos_ref, sin_ref, out_ref) = refs[:count], refs[count:]
    rows = jnp.concatenate([piece[...] for piece in pieces], axis=0)
    cosine = table_rows(cos_ref, slots, pieces[0].shape[0]) * QUERY_FACTOR
    sine = table_rows(sin_ref, slots, pieces[0].shape[0]) * QUERY_FACTOR
    step = min(weight_ref.shape[1], QUERY_COLS)

    @pl.loop(0, weight_ref.shape[1] // step)
    def _(tile):
        at = pl.multiple_of(tile * step, step)
        product = jnp.dot(rows, weight_ref[:, pl.ds(at, step)], preferred_element_type=jnp.float32)
        for head in range(0, step, HEAD_WIDTH):
            turned = turn(product[:, head : head + HEAD_WIDTH], cosine, sine)
            out_ref[:, pl.ds(at + head, HEAD_WIDTH)] = turned.astype(out_ref.dtype)


def query_rows(pieces, weight, cosine, sine, slots=None):
    rows = sum(piece.shape[0] for piece in pieces)
    return pl.pallas_call(
        functools.partial(query_kernel, slots),
        out_shape=jax.ShapeDtypeStruct((rows, weight.shape[1]), jnp.bfloat16),
        in_specs=[VMEM] * (len(pieces) + 3),
        out_specs=VMEM,
        compiler_params=params(18),
        cost_estimate=pl.CostEstimate(
            flops=2 * rows * weight.size, bytes_accessed=2 * weight.size, transcendentals=0
        ),
        name="query_rows",
    )(*pieces, weight, cosine, sine)


def attend_kernel(slots, held, placed, mask_ref, query_ref, kv_ref, weight_ref, *rest):
    out_refs, (live_ref, mixed_ref) = rest[: len(slots)], rest[len(slots) :]
    grp, core = lax.axis_index("grp"), lax.axis_index("blk") % 2
    piece_rows = query_ref.shape[0] // len(held)
    kv_heads = kv_ref.shape[1] // (2 * HEAD_WIDTH)
    repeat = query_ref.shape[1] // (kv_heads * HEAD_WIDTH)
    block = MASK_BLOCK_TOKENS

    for at, slot in enumerate(slots):
        query_piece = lax.bitwise_xor(grp, group_of(slot, core)) if placed else slot
        query_block = query_piece * piece_rows // block

        def note(index, count, query_block=query_block):
            live_ref[count] = index
            return count + mask_ref[query_block, index]

        count = lax.fori_loop(0, mask_ref.shape[1], note, jnp.int32(0), unroll=16)
        for spare in range(WIDE):
            live_ref[count + spare] = 0

        queries = [
            jnp.concatenate(
                [
                    query_ref[
                        held.index(slot) * piece_rows : (held.index(slot) + 1) * piece_rows,
                        (head * repeat + q) * HEAD_WIDTH : (head * repeat + q + 1) * HEAD_WIDTH,
                    ]
                    for q in range(repeat)
                ],
                axis=0,
            )
            for head in range(kv_heads)
        ]
        ones = jnp.ones((WIDE * block, HEAD_WIDTH), jnp.bfloat16)

        def step(index, state, queries=queries, count=count):
            first = index * WIDE
            starts = [
                pl.multiple_of(live_ref[first + wide] * block, block) for wide in range(WIDE)
            ]
            new_state = []
            for head, query in enumerate(queries):
                key_cols = slice(head * HEAD_WIDTH, (head + 1) * HEAD_WIDTH)
                value_cols = slice(
                    (kv_heads + head) * HEAD_WIDTH, (kv_heads + head + 1) * HEAD_WIDTH
                )
                keys = jnp.concatenate(
                    [kv_ref[pl.ds(start, block), key_cols] for start in starts], axis=0
                )
                values = jnp.concatenate(
                    [kv_ref[pl.ds(start, block), value_cols] for start in starts], axis=0
                )
                scores = lax.dot_general(
                    query, keys, (((1,), (1,)), ((), ())), preferred_element_type=jnp.float32
                )
                scores = jnp.concatenate(
                    [scores[:, : SURE * block]]
                    + [
                        scores[:, wide * block : (wide + 1) * block]
                        + jnp.where(first + wide < count, 0.0, NEG_FILL)
                        for wide in range(SURE, WIDE)
                    ],
                    axis=1,
                )
                top = jnp.max(scores, axis=1, keepdims=True)
                if state is not None:
                    top = jnp.maximum(state[2 * head], top)
                weights = jnp.exp2(scores - top).astype(jnp.bfloat16)
                sums = jnp.dot(
                    weights,
                    jnp.concatenate([values, ones], axis=1),
                    preferred_element_type=jnp.float32,
                )
                if state is not None:
                    sums = sums + state[2 * head + 1] * jnp.exp2(state[2 * head] - top)
                new_state += [top, sums]
            return tuple(new_state)

        state = lax.fori_loop(1, (count + WIDE - 1) // WIDE, step, step(0, None))
        for head in range(kv_heads):
            sums = state[2 * head + 1]
            mixed = (sums[:, :HEAD_WIDTH] / sums[:, HEAD_WIDTH:]).astype(jnp.bfloat16)
            for q in range(repeat):
                mixed_ref[
                    at * piece_rows : (at + 1) * piece_rows,
                    (head * repeat + q) * HEAD_WIDTH : (head * repeat + q + 1) * HEAD_WIDTH,
                ] = mixed[q * piece_rows : (q + 1) * piece_rows]

    tile_cols = weight_ref.shape[1] if mixed_ref.shape[0] <= 128 else 512

    @pl.loop(0, weight_ref.shape[1] // tile_cols)
    def _(tile):
        here = pl.ds(pl.multiple_of(tile * tile_cols, tile_cols), tile_cols)
        term = jnp.dot(
            mixed_ref[...], weight_ref[:, here], preferred_element_type=jnp.float32
        ).astype(jnp.bfloat16)
        for at in range(len(slots)):
            out_refs[at][:, here] = term[at * piece_rows : (at + 1) * piece_rows]


def gather_kernel(chunks, *refs):
    parts, out_ref = refs[:-1], refs[-1]
    grp, blk = lax.axis_index("grp"), lax.axis_index("blk")

    def place(owner, group, rows):
        at = (owner * 4 + group) * rows.shape[0]
        out_ref[pl.ds(pl.multiple_of(at, rows.shape[0]), rows.shape[0])] = rows

    at = 0
    for slots in chunks:
        shifts = parts[at].shape[0]
        piece_rows = parts[at].shape[1] // len(slots)
        for other in range(2):
            core = lax.bitwise_xor(blk % 2, other)
            for shift in range(shifts):
                owner = lax.bitwise_xor(blk // 2, chip_of(shift, shifts)) * 2 + core
                for index, slot in enumerate(slots):
                    group = lax.bitwise_xor(grp, group_of(slot, core))
                    rows = slice(index * piece_rows, (index + 1) * piece_rows)
                    place(owner, group, parts[at + other][shift, rows])
        at += 2


def gather_rows(chunks, parts, rows):
    return pl.pallas_call(
        functools.partial(gather_kernel, chunks),
        out_shape=jax.ShapeDtypeStruct((rows, parts[0].shape[-1]), jnp.bfloat16),
        in_specs=[VMEM] * len(parts),
        out_specs=VMEM,
        compiler_params=params(12),
        name="key_value_gather",
    )(*parts)


def attend(slots, held, placed, mask, query, kv, weight):
    piece_rows = query.shape[0] // len(held)
    term = jax.ShapeDtypeStruct((piece_rows, weight.shape[1]), jnp.bfloat16)
    return pl.pallas_call(
        functools.partial(attend_kernel, slots, held, placed),
        out_shape=[term] * len(slots),
        in_specs=[SMEM, VMEM, VMEM, VMEM],
        out_specs=[VMEM] * len(slots),
        scratch_shapes=[
            pltpu.SMEM((mask.shape[1] + 2 * WIDE,), jnp.int32),
            pltpu.VMEM((len(slots) * piece_rows, weight.shape[0]), jnp.bfloat16),
        ],
        compiler_params=params(20 if placed else 48),
        cost_estimate=pl.CostEstimate(
            flops=2 * len(slots) * piece_rows * weight.size * 2,
            bytes_accessed=2 * weight.size,
            transcendentals=0,
        ),
        name="attend_project",
    )(mask, query, kv, weight)


def rotary_tables(positions):
    half = HEAD_WIDTH // 2
    inverse = jnp.power(
        jnp.float32(ROPE_BASE),
        -(2.0 * (jnp.arange(HEAD_WIDTH) % half).astype(jnp.float32)) / HEAD_WIDTH,
    )
    sign = jnp.where(jnp.arange(HEAD_WIDTH) < half, -1.0, 1.0)
    angles = positions.astype(jnp.float32)[:, None] * inverse[None, :]
    return jnp.cos(angles), jnp.sin(angles) * sign[None, :]


def add(*values):
    total = values[0].astype(jnp.float32)
    for value in values[1:]:
        total = total + value.astype(jnp.float32)
    return total.astype(jnp.bfloat16)


def general_body(
    blk_count, groups, tokens, w_query, key_weight, value_weight, w_output, block_mask, positions
):
    rows = lax.all_gather(tokens, "grp", axis=0, tiled=True)
    cosine, sine = rotary_tables(positions)
    own = key_value_rows((rows,), key_weight, value_weight, cosine, sine)
    kv = lax.all_gather(own, "blk", axis=0, tiled=True)
    query = query_rows((rows,), w_query, cosine, sine)
    order = tuple(range(groups))
    terms = attend(order, order, False, block_mask, query, kv, w_output)
    term = jnp.concatenate(terms, axis=0)
    return lax.psum_scatter(term, "grp", scatter_dimension=0, tiled=True)


def square_body(
    blk_count, tokens, w_query, key_weight, value_weight, w_output, block_mask, positions
):
    chips = blk_count // 2

    def send(value, slot):
        pairs = []
        for g in range(4):
            for b in range(blk_count):
                pairs.append((g * blk_count + b, (g ^ group_of(slot, b % 2)) * blk_count + b))
        return lax.ppermute(value, ("grp", "blk"), pairs)

    first, second = send(tokens, 1), send(tokens, 2)
    across = send(first, 2)

    cosine, sine = rotary_tables(positions)
    key_weight, value_weight = preload((key_weight, value_weight), (cosine, sine))

    def exchange(slots, after=(), direct=True):
        own = key_value_rows(
            [pieces[slot] for slot in slots],
            kept(key_weight),
            kept(value_weight),
            cosine,
            sine,
            slots,
            after,
        )
        def across_chips(value, by):
            return lax.ppermute(value, "blk", [(b, b ^ (2 * by)) for b in range(blk_count)])

        near, far = across_chips(own, 1), across_chips(own, 3)
        if direct:
            last = across_chips(own, 2)
        else:
            near, far = lax.optimization_barrier((near, far))
            last = across_chips(far, 1)
        held = jnp.stack([own, far, near, last])
        return own, held

    def with_other_core(*held):
        held = jnp.concatenate(held, axis=1)
        return [held, lax.ppermute(held, "blk", [(b, b ^ 1) for b in range(blk_count)])]

    pieces = (tokens, first, second, across)
    rows_0, held_0 = exchange((0,), (), True)
    parts_0 = with_other_core(held_0)
    rows_1, held_1 = exchange((1, 2), parts_0, False)
    query_1 = query_rows(pieces[:3], w_query, cosine, sine, (0, 1, 2))
    rows_2, held_2 = exchange((3,), (rows_1, query_1), True)
    query_2 = query_rows(pieces[3:], w_query, cosine, sine, (3,))
    held_2, query_2 = lax.optimization_barrier((held_2, query_2))
    query = {(0, 1, 2): query_1, (3,): query_2}
    parts = parts_0 + with_other_core(held_1, held_2)
    chunks = ((0,), (1, 2, 3))
    kv = gather_rows(chunks, parts, blk_count * positions.shape[0])

    def terms(slots):
        held = next(held for held in query if slots[0] in held)
        return attend(slots, held, True, block_mask, query[held], kv, w_output)

    (term_across,) = terms((3,))
    sent_across = send(term_across, 2)
    term_first, term_second = terms((1, 2))
    sent_second = send(term_second, 2)
    sent_first = send(add(term_first, sent_across), 1)
    (term_own,) = terms((0,))
    return add(term_own, sent_second, sent_first)


def solution(mesh):
    groups, blk_count = mesh.shape["grp"], mesh.shape["blk"]
    if groups == 4 and blk_count == 8:
        body = functools.partial(square_body, blk_count)
    else:
        body = functools.partial(general_body, blk_count, groups)
    return jax.shard_map(
        body,
        mesh=mesh,
        in_specs=(
            P(("blk", "grp"), None),
            P(None, "grp"),
            P(None, "grp"),
            P(None, "grp"),
            P("grp", None),
            P("blk", None),
            P("blk"),
        ),
        out_specs=P(("blk", "grp"), None),
        check_vma=False,
    )
```

```python
import functools
import math

import jax
import jax.numpy as jnp
from jax import lax
from jax.experimental import pallas as pl
from jax.experimental.pallas import tpu as pltpu
from jax.sharding import PartitionSpec as P

HEAD_WIDTH = 128
MASK_BLOCK_TOKENS = 128
ROPE_BASE = 500000.0
NEG_FILL = -1e30
QUERY_COLS = 1024
WIDE = 8
SURE = 6
QUERY_FACTOR = HEAD_WIDTH**-0.5 * math.log2(math.e)
ANY = pl.BlockSpec(memory_space=pl.ANY)
VMEM = pl.BlockSpec(memory_space=pltpu.VMEM)
SMEM = pl.BlockSpec(memory_space=pltpu.SMEM)
MIB = 1 << 20


def params(mib):
    return pltpu.CompilerParams(vmem_limit_bytes=mib * MIB)


def turn(product, cosine, sine):
    return product * cosine + pltpu.roll(product, HEAD_WIDTH // 2, 1) * sine


def preload_kernel(count, *refs):
    sources, targets, sems = refs[:count], refs[-1 - count : -1], refs[-1]
    copies = [
        pltpu.make_async_copy(source, target, sems.at[at])
        for at, (source, target) in enumerate(zip(sources, targets))
    ]
    for copy in copies:
        copy.start()
    for copy in copies:
        copy.wait()


def preload(weights, after):
    return pl.pallas_call(
        functools.partial(preload_kernel, len(weights)),
        out_shape=[pltpu.VMEM(weight.shape, weight.dtype) for weight in weights],
        in_specs=[ANY] * (len(weights) + len(after)),
        out_specs=[VMEM] * len(weights),
        scratch_shapes=[pltpu.SemaphoreType.DMA((len(weights),))],
        compiler_params=params(1),
        name="preload",
    )(*[pltpu.with_memory_space_constraint(weight, pltpu.HBM) for weight in weights], *after)


def kept(weight):
    return pltpu.with_memory_space_constraint(weight, pltpu.VMEM)


def group_of(slot, core):
    return {0: 0, 1: 1 + core, 2: 2 - core, 3: 3}[slot]


def chip_of(at, chips):
    shift, step, place = 0, chips // 2, 1
    while step:
        shift = shift ^ ((at // place % 2) * (2 * step - 1))
        step, place = step // 2, place * 2
    return shift


def table_rows(ref, slots, piece_rows):
    if slots is None:
        return ref[...]
    grp, core = lax.axis_index("grp"), lax.axis_index("blk") % 2
    rows = []
    for slot in slots:
        at = lax.bitwise_xor(grp, group_of(slot, core)) * piece_rows
        rows.append(ref[pl.ds(pl.multiple_of(at, piece_rows), piece_rows)])
    return jnp.concatenate(rows, axis=0)


def key_value_kernel(count, slots, *refs):
    pieces, (key_ref, value_ref, cos_ref, sin_ref, *_, out_ref) = refs[:count], refs[count:]
    width = key_ref.shape[1]
    rows = jnp.concatenate([piece[...] for piece in pieces], axis=0)
    keys = jnp.dot(rows, key_ref[...], preferred_element_type=jnp.float32)
    values = jnp.dot(rows, value_ref[...], preferred_element_type=jnp.float32)
    cosine = table_rows(cos_ref, slots, pieces[0].shape[0])
    sine = table_rows(sin_ref, slots, pieces[0].shape[0])
    for at in range(0, width, HEAD_WIDTH):
        head = slice(at, at + HEAD_WIDTH)
        out_ref[:, head] = turn(keys[:, head], cosine, sine).astype(out_ref.dtype)
    out_ref[:, width:] = values.astype(out_ref.dtype)


def key_value_rows(
    pieces, key_weight, value_weight, cosine, sine, slots=None, after=(), weigh=1
):
    rows = sum(piece.shape[0] for piece in pieces)
    width = key_weight.shape[1] + value_weight.shape[1]
    return pl.pallas_call(
        functools.partial(key_value_kernel, len(pieces), slots),
        out_shape=jax.ShapeDtypeStruct((rows, width), jnp.bfloat16),
        in_specs=[VMEM] * (len(pieces) + 4) + [ANY] * len(after),
        out_specs=VMEM,
        compiler_params=params(16),
        cost_estimate=pl.CostEstimate(
            flops=2 * rows * (key_weight.size + value_weight.size) * weigh,
            bytes_accessed=2 * (key_weight.size + value_weight.size),
            transcendentals=0,
        ),
        name="key_value_rows",
    )(*pieces, key_weight, value_weight, cosine, sine, *after)


def query_kernel(slots, *refs):
    count = len(refs) - 4
    pieces, (weight_ref, cos_ref, sin_ref, out_ref) = refs[:count], refs[count:]
    rows = jnp.concatenate([piece[...] for piece in pieces], axis=0)
    cosine = table_rows(cos_ref, slots, pieces[0].shape[0]) * QUERY_FACTOR
    sine = table_rows(sin_ref, slots, pieces[0].shape[0]) * QUERY_FACTOR
    step = min(weight_ref.shape[1], QUERY_COLS)

    @pl.loop(0, weight_ref.shape[1] // step)
    def _(tile):
        at = pl.multiple_of(tile * step, step)
        product = jnp.dot(rows, weight_ref[:, pl.ds(at, step)], preferred_element_type=jnp.float32)
        for head in range(0, step, HEAD_WIDTH):
            turned = turn(product[:, head : head + HEAD_WIDTH], cosine, sine)
            out_ref[:, pl.ds(at + head, HEAD_WIDTH)] = turned.astype(out_ref.dtype)


def query_rows(pieces, weight, cosine, sine, slots=None):
    rows = sum(piece.shape[0] for piece in pieces)
    return pl.pallas_call(
        functools.partial(query_kernel, slots),
        out_shape=jax.ShapeDtypeStruct((rows, weight.shape[1]), jnp.bfloat16),
        in_specs=[VMEM] * (len(pieces) + 3),
        out_specs=VMEM,
        compiler_params=params(18),
        cost_estimate=pl.CostEstimate(
            flops=2 * rows * weight.size, bytes_accessed=2 * weight.size, transcendentals=0
        ),
        name="query_rows",
    )(*pieces, weight, cosine, sine)


def attend_kernel(slots, held, placed, mask_ref, query_ref, kv_ref, weight_ref, *rest):
    out_refs, (live_ref, mixed_ref) = rest[: len(slots)], rest[len(slots) :]
    grp, core = lax.axis_index("grp"), lax.axis_index("blk") % 2
    piece_rows = query_ref.shape[0] // len(held)
    kv_heads = kv_ref.shape[1] // (2 * HEAD_WIDTH)
    repeat = query_ref.shape[1] // (kv_heads * HEAD_WIDTH)
    block = MASK_BLOCK_TOKENS

    for at, slot in enumerate(slots):
        query_piece = lax.bitwise_xor(grp, group_of(slot, core)) if placed else slot
        query_block = query_piece * piece_rows // block

        def note(index, count, query_block=query_block):
            live_ref[count] = index
            return count + mask_ref[query_block, index]

        count = lax.fori_loop(0, mask_ref.shape[1], note, jnp.int32(0), unroll=16)
        for spare in range(WIDE):
            live_ref[count + spare] = 0

        queries = [
            jnp.concatenate(
                [
                    query_ref[
                        held.index(slot) * piece_rows : (held.index(slot) + 1) * piece_rows,
                        (head * repeat + q) * HEAD_WIDTH : (head * repeat + q + 1) * HEAD_WIDTH,
                    ]
                    for q in range(repeat)
                ],
                axis=0,
            )
            for head in range(kv_heads)
        ]
        ones = jnp.ones((WIDE * block, HEAD_WIDTH), jnp.bfloat16)

        def step(index, state, queries=queries, count=count):
            first = index * WIDE
            starts = [
                pl.multiple_of(live_ref[first + wide] * block, block) for wide in range(WIDE)
            ]
            new_state = []
            for head, query in enumerate(queries):
                key_cols = slice(head * HEAD_WIDTH, (head + 1) * HEAD_WIDTH)
                value_cols = slice(
                    (kv_heads + head) * HEAD_WIDTH, (kv_heads + head + 1) * HEAD_WIDTH
                )
                keys = jnp.concatenate(
                    [kv_ref[pl.ds(start, block), key_cols] for start in starts], axis=0
                )
                values = jnp.concatenate(
                    [kv_ref[pl.ds(start, block), value_cols] for start in starts], axis=0
                )
                scores = lax.dot_general(
                    query, keys, (((1,), (1,)), ((), ())), preferred_element_type=jnp.float32
                )
                scores = jnp.concatenate(
                    [scores[:, : SURE * block]]
                    + [
                        scores[:, wide * block : (wide + 1) * block]
                        + jnp.where(first + wide < count, 0.0, NEG_FILL)
                        for wide in range(SURE, WIDE)
                    ],
                    axis=1,
                )
                top = jnp.max(scores, axis=1, keepdims=True)
                if state is not None:
                    top = jnp.maximum(state[2 * head], top)
                weights = jnp.exp2(scores - top).astype(jnp.bfloat16)
                sums = jnp.dot(
                    weights,
                    jnp.concatenate([values, ones], axis=1),
                    preferred_element_type=jnp.float32,
                )
                if state is not None:
                    sums = sums + state[2 * head + 1] * jnp.exp2(state[2 * head] - top)
                new_state += [top, sums]
            return tuple(new_state)

        def many_steps(step=step, count=count):
            one, two = step(0, None), step(1, None)
            state = []
            for head in range(kv_heads):
                top = jnp.maximum(one[2 * head], two[2 * head])
                state += [
                    top,
                    one[2 * head + 1] * jnp.exp2(one[2 * head] - top)
                    + two[2 * head + 1] * jnp.exp2(two[2 * head] - top),
                ]
            return lax.fori_loop(2, (count + WIDE - 1) // WIDE, step, tuple(state))

        state = lax.cond(count > WIDE, many_steps, functools.partial(step, 0, None))
        for head in range(kv_heads):
            sums = state[2 * head + 1]
            mixed = (sums[:, :HEAD_WIDTH] / sums[:, HEAD_WIDTH:]).astype(jnp.bfloat16)
            for q in range(repeat):
                mixed_ref[
                    at * piece_rows : (at + 1) * piece_rows,
                    (head * repeat + q) * HEAD_WIDTH : (head * repeat + q + 1) * HEAD_WIDTH,
                ] = mixed[q * piece_rows : (q + 1) * piece_rows]

    tile_cols = weight_ref.shape[1] if mixed_ref.shape[0] <= 128 else 512

    @pl.loop(0, weight_ref.shape[1] // tile_cols)
    def _(tile):
        here = pl.ds(pl.multiple_of(tile * tile_cols, tile_cols), tile_cols)
        term = jnp.dot(
            mixed_ref[...], weight_ref[:, here], preferred_element_type=jnp.float32
        ).astype(jnp.bfloat16)
        for at in range(len(slots)):
            out_refs[at][:, here] = term[at * piece_rows : (at + 1) * piece_rows]


def gather_kernel(chunks, *refs):
    parts, out_ref = refs[:-1], refs[-1]
    grp, blk = lax.axis_index("grp"), lax.axis_index("blk")

    def place(owner, group, rows):
        at = (owner * 4 + group) * rows.shape[0]
        out_ref[pl.ds(pl.multiple_of(at, rows.shape[0]), rows.shape[0])] = rows

    at = 0
    for slots in chunks:
        shifts = parts[at].shape[0]
        piece_rows = parts[at].shape[1] // len(slots)
        for other in range(2):
            core = lax.bitwise_xor(blk % 2, other)
            for shift in range(shifts):
                owner = lax.bitwise_xor(blk // 2, chip_of(shift, shifts)) * 2 + core
                for index, slot in enumerate(slots):
                    group = lax.bitwise_xor(grp, group_of(slot, core))
                    rows = slice(index * piece_rows, (index + 1) * piece_rows)
                    place(owner, group, parts[at + other][shift, rows])
        at += 2


def gather_rows(chunks, parts, rows):
    return pl.pallas_call(
        functools.partial(gather_kernel, chunks),
        out_shape=jax.ShapeDtypeStruct((rows, parts[0].shape[-1]), jnp.bfloat16),
        in_specs=[VMEM] * len(parts),
        out_specs=VMEM,
        compiler_params=params(12),
        name="key_value_gather",
    )(*parts)


def attend(slots, held, placed, mask, query, kv, weight):
    piece_rows = query.shape[0] // len(held)
    term = jax.ShapeDtypeStruct((piece_rows, weight.shape[1]), jnp.bfloat16)
    return pl.pallas_call(
        functools.partial(attend_kernel, slots, held, placed),
        out_shape=[term] * len(slots),
        in_specs=[SMEM, VMEM, VMEM, VMEM],
        out_specs=[VMEM] * len(slots),
        scratch_shapes=[
            pltpu.SMEM((mask.shape[1] + 2 * WIDE,), jnp.int32),
            pltpu.VMEM((len(slots) * piece_rows, weight.shape[0]), jnp.bfloat16),
        ],
        compiler_params=params(20 if placed else 48),
        cost_estimate=pl.CostEstimate(
            flops=2 * len(slots) * piece_rows * weight.size * 2,
            bytes_accessed=2 * weight.size,
            transcendentals=0,
        ),
        name="attend_project",
    )(mask, query, kv, weight)


def rotary_tables(positions):
    half = HEAD_WIDTH // 2
    inverse = jnp.power(
        jnp.float32(ROPE_BASE),
        -(2.0 * (jnp.arange(HEAD_WIDTH) % half).astype(jnp.float32)) / HEAD_WIDTH,
    )
    sign = jnp.where(jnp.arange(HEAD_WIDTH) < half, -1.0, 1.0)
    angles = positions.astype(jnp.float32)[:, None] * inverse[None, :]
    return jnp.cos(angles), jnp.sin(angles) * sign[None, :]


def add(*values):
    total = values[0].astype(jnp.float32)
    for value in values[1:]:
        total = total + value.astype(jnp.float32)
    return total.astype(jnp.bfloat16)


def general_body(
    blk_count, groups, tokens, w_query, key_weight, value_weight, w_output, block_mask, positions
):
    rows = lax.all_gather(tokens, "grp", axis=0, tiled=True)
    cosine, sine = rotary_tables(positions)
    own = key_value_rows((rows,), key_weight, value_weight, cosine, sine)
    kv = lax.all_gather(own, "blk", axis=0, tiled=True)
    query = query_rows((rows,), w_query, cosine, sine)
    order = tuple(range(groups))
    terms = attend(order, order, False, block_mask, query, kv, w_output)
    term = jnp.concatenate(terms, axis=0)
    return lax.psum_scatter(term, "grp", scatter_dimension=0, tiled=True)


def square_body(
    blk_count, tokens, w_query, key_weight, value_weight, w_output, block_mask, positions
):
    chips = blk_count // 2

    def send(value, slot):
        pairs = []
        for g in range(4):
            for b in range(blk_count):
                pairs.append((g * blk_count + b, (g ^ group_of(slot, b % 2)) * blk_count + b))
        return lax.ppermute(value, ("grp", "blk"), pairs)

    first, second = send(tokens, 1), send(tokens, 2)
    across = send(first, 2)

    cosine, sine = rotary_tables(positions)
    key_weight, value_weight = preload((key_weight, value_weight), (cosine, sine))

    def exchange(slots, after=(), direct=True):
        own = key_value_rows(
            [pieces[slot] for slot in slots],
            kept(key_weight),
            kept(value_weight),
            cosine,
            sine,
            slots,
            after,
        )
        def across_chips(value, by):
            return lax.ppermute(value, "blk", [(b, b ^ (2 * by)) for b in range(blk_count)])

        near, far = across_chips(own, 1), across_chips(own, 3)
        if direct:
            last = across_chips(own, 2)
        else:
            near, far = lax.optimization_barrier((near, far))
            last = across_chips(far, 1)
        held = jnp.stack([own, far, near, last])
        return own, held

    def with_other_core(*held):
        held = jnp.concatenate(held, axis=1)
        return [held, lax.ppermute(held, "blk", [(b, b ^ 1) for b in range(blk_count)])]

    pieces = (tokens, first, second, across)
    rows_0, held_0 = exchange((0,), (), True)
    parts_0 = with_other_core(held_0)
    rows_1, held_1 = exchange((1, 2), parts_0, False)
    query_1 = query_rows(pieces[:3], w_query, cosine, sine, (0, 1, 2))
    rows_2, held_2 = exchange((3,), (rows_1, query_1), True)
    query_2 = query_rows(pieces[3:], w_query, cosine, sine, (3,))
    held_2, query_2 = lax.optimization_barrier((held_2, query_2))
    query = {(0, 1, 2): query_1, (3,): query_2}
    parts = parts_0 + with_other_core(held_1, held_2)
    chunks = ((0,), (1, 2, 3))
    kv = gather_rows(chunks, parts, blk_count * positions.shape[0])

    def terms(slots):
        held = next(held for held in query if slots[0] in held)
        return attend(slots, held, True, block_mask, query[held], kv, w_output)

    (term_across,) = terms((3,))
    sent_across = send(term_across, 2)
    term_first, term_second = terms((1, 2))
    sent_second = send(term_second, 2)
    sent_first = send(add(term_first, sent_across), 1)
    (term_own,) = terms((0,))
    return add(term_own, sent_second, sent_first)


def solution(mesh):
    groups, blk_count = mesh.shape["grp"], mesh.shape["blk"]
    if groups == 4 and blk_count == 8:
        body = functools.partial(square_body, blk_count)
    else:
        body = functools.partial(general_body, blk_count, groups)
    return jax.shard_map(
        body,
        mesh=mesh,
        in_specs=(
            P(("blk", "grp"), None),
            P(None, "grp"),
            P(None, "grp"),
            P(None, "grp"),
            P("grp", None),
            P("blk", None),
            P("blk"),
        ),
        out_specs=P(("blk", "grp"), None),
        check_vma=False,
    )
```

```python
import functools
import math

import jax
import jax.numpy as jnp
from jax import lax
from jax.experimental import pallas as pl
from jax.experimental.pallas import tpu as pltpu
from jax.sharding import PartitionSpec as P

HEAD_WIDTH = 128
MASK_BLOCK_TOKENS = 128
ROPE_BASE = 500000.0
NEG_FILL = -1e30
QUERY_COLS = 1024
WIDE = 8
SURE = 6
QUERY_FACTOR = HEAD_WIDTH**-0.5 * math.log2(math.e)
ANY = pl.BlockSpec(memory_space=pl.ANY)
VMEM = pl.BlockSpec(memory_space=pltpu.VMEM)
SMEM = pl.BlockSpec(memory_space=pltpu.SMEM)
MIB = 1 << 20


def params(mib):
    return pltpu.CompilerParams(vmem_limit_bytes=mib * MIB)


def turn(product, cosine, sine):
    return product * cosine + pltpu.roll(product, HEAD_WIDTH // 2, 1) * sine


def preload_kernel(count, *refs):
    sources, targets, sems = refs[:count], refs[-1 - count : -1], refs[-1]
    copies = [
        pltpu.make_async_copy(source, target, sems.at[at])
        for at, (source, target) in enumerate(zip(sources, targets))
    ]
    for copy in copies:
        copy.start()
    for copy in copies:
        copy.wait()


def preload(weights, after):
    return pl.pallas_call(
        functools.partial(preload_kernel, len(weights)),
        out_shape=[pltpu.VMEM(weight.shape, weight.dtype) for weight in weights],
        in_specs=[ANY] * (len(weights) + len(after)),
        out_specs=[VMEM] * len(weights),
        scratch_shapes=[pltpu.SemaphoreType.DMA((len(weights),))],
        compiler_params=params(1),
        name="preload",
    )(*[pltpu.with_memory_space_constraint(weight, pltpu.HBM) for weight in weights], *after)


def kept(weight):
    return pltpu.with_memory_space_constraint(weight, pltpu.VMEM)


def group_of(slot, core):
    return {0: 0, 1: 1 + core, 2: 2 - core, 3: 3}[slot]


def chip_of(at, chips):
    shift, step, place = 0, chips // 2, 1
    while step:
        shift = shift ^ ((at // place % 2) * (2 * step - 1))
        step, place = step // 2, place * 2
    return shift


def table_rows(ref, slots, piece_rows):
    if slots is None:
        return ref[...]
    grp, core = lax.axis_index("grp"), lax.axis_index("blk") % 2
    rows = []
    for slot in slots:
        at = lax.bitwise_xor(grp, group_of(slot, core)) * piece_rows
        rows.append(ref[pl.ds(pl.multiple_of(at, piece_rows), piece_rows)])
    return jnp.concatenate(rows, axis=0)


def key_value_kernel(count, slots, *refs):
    pieces, (key_ref, value_ref, cos_ref, sin_ref, *_, out_ref) = refs[:count], refs[count:]
    width = key_ref.shape[1]
    rows = jnp.concatenate([piece[...] for piece in pieces], axis=0)
    keys = jnp.dot(rows, key_ref[...], preferred_element_type=jnp.float32)
    values = jnp.dot(rows, value_ref[...], preferred_element_type=jnp.float32)
    cosine = table_rows(cos_ref, slots, pieces[0].shape[0])
    sine = table_rows(sin_ref, slots, pieces[0].shape[0])
    for at in range(0, width, HEAD_WIDTH):
        head = slice(at, at + HEAD_WIDTH)
        out_ref[:, head] = turn(keys[:, head], cosine, sine).astype(out_ref.dtype)
    out_ref[:, width:] = values.astype(out_ref.dtype)


def key_value_rows(
    pieces, key_weight, value_weight, cosine, sine, slots=None, after=(), weigh=1
):
    rows = sum(piece.shape[0] for piece in pieces)
    width = key_weight.shape[1] + value_weight.shape[1]
    return pl.pallas_call(
        functools.partial(key_value_kernel, len(pieces), slots),
        out_shape=jax.ShapeDtypeStruct((rows, width), jnp.bfloat16),
        in_specs=[VMEM] * (len(pieces) + 4) + [ANY] * len(after),
        out_specs=VMEM,
        compiler_params=params(16),
        cost_estimate=pl.CostEstimate(
            flops=2 * rows * (key_weight.size + value_weight.size) * weigh,
            bytes_accessed=2 * (key_weight.size + value_weight.size),
            transcendentals=0,
        ),
        name="key_value_rows",
    )(*pieces, key_weight, value_weight, cosine, sine, *after)


def query_kernel(slots, *refs):
    count = len(refs) - 4
    pieces, (weight_ref, cos_ref, sin_ref, out_ref) = refs[:count], refs[count:]
    rows = jnp.concatenate([piece[...] for piece in pieces], axis=0)
    cosine = table_rows(cos_ref, slots, pieces[0].shape[0]) * QUERY_FACTOR
    sine = table_rows(sin_ref, slots, pieces[0].shape[0]) * QUERY_FACTOR
    step = min(weight_ref.shape[1], QUERY_COLS)

    @pl.loop(0, weight_ref.shape[1] // step)
    def _(tile):
        at = pl.multiple_of(tile * step, step)
        product = jnp.dot(rows, weight_ref[:, pl.ds(at, step)], preferred_element_type=jnp.float32)
        for head in range(0, step, HEAD_WIDTH):
            turned = turn(product[:, head : head + HEAD_WIDTH], cosine, sine)
            out_ref[:, pl.ds(at + head, HEAD_WIDTH)] = turned.astype(out_ref.dtype)


def query_rows(pieces, weight, cosine, sine, slots=None):
    rows = sum(piece.shape[0] for piece in pieces)
    return pl.pallas_call(
        functools.partial(query_kernel, slots),
        out_shape=jax.ShapeDtypeStruct((rows, weight.shape[1]), jnp.bfloat16),
        in_specs=[VMEM] * (len(pieces) + 3),
        out_specs=VMEM,
        compiler_params=params(18),
        cost_estimate=pl.CostEstimate(
            flops=2 * rows * weight.size, bytes_accessed=2 * weight.size, transcendentals=0
        ),
        name="query_rows",
    )(*pieces, weight, cosine, sine)


def attend_kernel(slots, held, placed, mask_ref, query_ref, kv_ref, weight_ref, *rest):
    out_refs, (live_ref, mixed_ref) = rest[: len(slots)], rest[len(slots) :]
    grp, core = lax.axis_index("grp"), lax.axis_index("blk") % 2
    piece_rows = query_ref.shape[0] // len(held)
    kv_heads = kv_ref.shape[1] // (2 * HEAD_WIDTH)
    repeat = query_ref.shape[1] // (kv_heads * HEAD_WIDTH)
    block = MASK_BLOCK_TOKENS

    for at, slot in enumerate(slots):
        query_piece = lax.bitwise_xor(grp, group_of(slot, core)) if placed else slot
        query_block = query_piece * piece_rows // block

        def note(index, count, query_block=query_block):
            live_ref[count] = index
            return count + mask_ref[query_block, index]

        count = lax.fori_loop(0, mask_ref.shape[1], note, jnp.int32(0), unroll=16)
        for spare in range(WIDE):
            live_ref[count + spare] = 0

        queries = [
            jnp.concatenate(
                [
                    query_ref[
                        held.index(slot) * piece_rows : (held.index(slot) + 1) * piece_rows,
                        (head * repeat + q) * HEAD_WIDTH : (head * repeat + q + 1) * HEAD_WIDTH,
                    ]
                    for q in range(repeat)
                ],
                axis=0,
            )
            for head in range(kv_heads)
        ]
        ones = jnp.ones((WIDE * block, HEAD_WIDTH), jnp.bfloat16)

        def step(index, state, queries=queries, count=count):
            first = index * WIDE
            starts = [
                pl.multiple_of(live_ref[first + wide] * block, block) for wide in range(WIDE)
            ]
            new_state = []
            for head, query in enumerate(queries):
                key_cols = slice(head * HEAD_WIDTH, (head + 1) * HEAD_WIDTH)
                value_cols = slice(
                    (kv_heads + head) * HEAD_WIDTH, (kv_heads + head + 1) * HEAD_WIDTH
                )
                keys = jnp.concatenate(
                    [kv_ref[pl.ds(start, block), key_cols] for start in starts], axis=0
                )
                values = jnp.concatenate(
                    [kv_ref[pl.ds(start, block), value_cols] for start in starts], axis=0
                )
                scores = lax.dot_general(
                    query, keys, (((1,), (1,)), ((), ())), preferred_element_type=jnp.float32
                )
                scores = jnp.concatenate(
                    [scores[:, : SURE * block]]
                    + [
                        scores[:, wide * block : (wide + 1) * block]
                        + jnp.where(first + wide < count, 0.0, NEG_FILL)
                        for wide in range(SURE, WIDE)
                    ],
                    axis=1,
                )
                top = jnp.max(scores, axis=1, keepdims=True)
                if state is not None:
                    top = jnp.maximum(state[2 * head], top)
                weights = jnp.exp2(scores - top).astype(jnp.bfloat16)
                sums = jnp.dot(
                    weights,
                    jnp.concatenate([values, ones], axis=1),
                    preferred_element_type=jnp.float32,
                )
                if state is not None:
                    sums = sums + state[2 * head + 1] * jnp.exp2(state[2 * head] - top)
                new_state += [top, sums]
            return tuple(new_state)

        def many_steps(step=step, count=count):
            one, two = step(0, None), step(1, None)
            state = []
            for head in range(kv_heads):
                top = jnp.maximum(one[2 * head], two[2 * head])
                state += [
                    top,
                    one[2 * head + 1] * jnp.exp2(one[2 * head] - top)
                    + two[2 * head + 1] * jnp.exp2(two[2 * head] - top),
                ]
            return lax.fori_loop(2, (count + WIDE - 1) // WIDE, step, tuple(state))

        state = lax.cond(count > WIDE, many_steps, functools.partial(step, 0, None))
        for head in range(kv_heads):
            sums = state[2 * head + 1]
            mixed = (sums[:, :HEAD_WIDTH] / sums[:, HEAD_WIDTH:]).astype(jnp.bfloat16)
            for q in range(repeat):
                mixed_ref[
                    at * piece_rows : (at + 1) * piece_rows,
                    (head * repeat + q) * HEAD_WIDTH : (head * repeat + q + 1) * HEAD_WIDTH,
                ] = mixed[q * piece_rows : (q + 1) * piece_rows]

    tile_cols = weight_ref.shape[1] if mixed_ref.shape[0] <= 128 else 512

    @pl.loop(0, weight_ref.shape[1] // tile_cols)
    def _(tile):
        here = pl.ds(pl.multiple_of(tile * tile_cols, tile_cols), tile_cols)
        term = jnp.dot(
            mixed_ref[...], weight_ref[:, here], preferred_element_type=jnp.float32
        ).astype(jnp.bfloat16)
        for at in range(len(slots)):
            out_refs[at][:, here] = term[at * piece_rows : (at + 1) * piece_rows]


def gather_kernel(chunks, *refs):
    parts, out_ref = refs[:-1], refs[-1]
    grp, blk = lax.axis_index("grp"), lax.axis_index("blk")

    def place(owner, group, rows):
        at = (owner * 4 + group) * rows.shape[0]
        out_ref[pl.ds(pl.multiple_of(at, rows.shape[0]), rows.shape[0])] = rows

    at = 0
    for slots in chunks:
        shifts = parts[at].shape[0]
        piece_rows = parts[at].shape[1] // len(slots)
        for other in range(2):
            core = lax.bitwise_xor(blk % 2, other)
            for shift in range(shifts):
                owner = lax.bitwise_xor(blk // 2, chip_of(shift, shifts)) * 2 + core
                for index, slot in enumerate(slots):
                    group = lax.bitwise_xor(grp, group_of(slot, core))
                    rows = slice(index * piece_rows, (index + 1) * piece_rows)
                    place(owner, group, parts[at + other][shift, rows])
        at += 2


def gather_rows(chunks, parts, rows):
    return pl.pallas_call(
        functools.partial(gather_kernel, chunks),
        out_shape=jax.ShapeDtypeStruct((rows, parts[0].shape[-1]), jnp.bfloat16),
        in_specs=[VMEM] * len(parts),
        out_specs=VMEM,
        compiler_params=params(12),
        name="key_value_gather",
    )(*parts)


def attend(slots, held, placed, mask, query, kv, weight):
    piece_rows = query.shape[0] // len(held)
    term = jax.ShapeDtypeStruct((piece_rows, weight.shape[1]), jnp.bfloat16)
    return pl.pallas_call(
        functools.partial(attend_kernel, slots, held, placed),
        out_shape=[term] * len(slots),
        in_specs=[SMEM, VMEM, VMEM, VMEM],
        out_specs=[VMEM] * len(slots),
        scratch_shapes=[
            pltpu.SMEM((mask.shape[1] + 2 * WIDE,), jnp.int32),
            pltpu.VMEM((len(slots) * piece_rows, weight.shape[0]), jnp.bfloat16),
        ],
        compiler_params=params(20 if placed else 48),
        cost_estimate=pl.CostEstimate(
            flops=2 * len(slots) * piece_rows * weight.size * 2,
            bytes_accessed=2 * weight.size,
            transcendentals=0,
        ),
        name="attend_project",
    )(mask, query, kv, weight)


def rotary_tables(positions):
    half = HEAD_WIDTH // 2
    inverse = jnp.power(
        jnp.float32(ROPE_BASE),
        -(2.0 * (jnp.arange(HEAD_WIDTH) % half).astype(jnp.float32)) / HEAD_WIDTH,
    )
    sign = jnp.where(jnp.arange(HEAD_WIDTH) < half, -1.0, 1.0)
    angles = positions.astype(jnp.float32)[:, None] * inverse[None, :]
    return jnp.cos(angles), jnp.sin(angles) * sign[None, :]


def add(*values):
    total = values[0].astype(jnp.float32)
    for value in values[1:]:
        total = total + value.astype(jnp.float32)
    return total.astype(jnp.bfloat16)


def general_body(
    blk_count, groups, tokens, w_query, key_weight, value_weight, w_output, block_mask, positions
):
    rows = lax.all_gather(tokens, "grp", axis=0, tiled=True)
    cosine, sine = rotary_tables(positions)
    own = key_value_rows((rows,), key_weight, value_weight, cosine, sine)
    kv = lax.all_gather(own, "blk", axis=0, tiled=True)
    query = query_rows((rows,), w_query, cosine, sine)
    order = tuple(range(groups))
    terms = attend(order, order, False, block_mask, query, kv, w_output)
    term = jnp.concatenate(terms, axis=0)
    return lax.psum_scatter(term, "grp", scatter_dimension=0, tiled=True)


def square_body(
    blk_count, tokens, w_query, key_weight, value_weight, w_output, block_mask, positions
):
    chips = blk_count // 2

    def send(value, slot):
        pairs = []
        for g in range(4):
            for b in range(blk_count):
                pairs.append((g * blk_count + b, (g ^ group_of(slot, b % 2)) * blk_count + b))
        return lax.ppermute(value, ("grp", "blk"), pairs)

    first, second = send(tokens, 1), send(tokens, 2)
    across = send(first, 2)

    cosine, sine = rotary_tables(positions)
    key_weight, value_weight = preload((key_weight, value_weight), (cosine, sine))

    def exchange(slots, after=(), direct=True):
        own = key_value_rows(
            [pieces[slot] for slot in slots],
            kept(key_weight),
            kept(value_weight),
            cosine,
            sine,
            slots,
            after,
        )
        def across_chips(value, by):
            return lax.ppermute(value, "blk", [(b, b ^ (2 * by)) for b in range(blk_count)])

        near, far = across_chips(own, 1), across_chips(own, 3)
        if direct:
            last = across_chips(own, 2)
        else:
            near, far = lax.optimization_barrier((near, far))
            last = across_chips(far, 1)
        held = jnp.stack([own, far, near, last])
        return own, held

    def with_other_core(*held):
        held = jnp.concatenate(held, axis=1)
        return [held, lax.ppermute(held, "blk", [(b, b ^ 1) for b in range(blk_count)])]

    pieces = (tokens, first, second, across)
    rows_0, held_0 = exchange((0,), (), True)
    parts_0 = with_other_core(held_0)
    rows_1, held_1 = exchange((1, 2), parts_0, False)
    query_1 = query_rows(pieces[:3], w_query, cosine, sine, (0, 1, 2))
    rows_2, held_2 = exchange((3,), (rows_1, query_1), True)
    query_2 = query_rows(pieces[3:], w_query, cosine, sine, (3,))
    held_2, query_2 = lax.optimization_barrier((held_2, query_2))
    query = {(0, 1, 2): query_1, (3,): query_2}
    parts = parts_0 + with_other_core(held_1, held_2)
    chunks = ((0,), (1, 2, 3))
    kv = gather_rows(chunks, parts, blk_count * positions.shape[0])

    def terms(slots):
        held = next(held for held in query if slots[0] in held)
        return attend(slots, held, True, block_mask, query[held], kv, w_output)

    (term_across,) = terms((3,))
    sent_across = send(term_across, 2)
    (term_second,) = terms((2,))
    sent_second = send(term_second, 2)
    (term_first,) = terms((1,))
    sent_first = send(add(term_first, sent_across), 1)
    (term_own,) = terms((0,))
    return add(term_own, sent_second, sent_first)


def solution(mesh):
    groups, blk_count = mesh.shape["grp"], mesh.shape["blk"]
    if groups == 4 and blk_count == 8:
        body = functools.partial(square_body, blk_count)
    else:
        body = functools.partial(general_body, blk_count, groups)
    return jax.shard_map(
        body,
        mesh=mesh,
        in_specs=(
            P(("blk", "grp"), None),
            P(None, "grp"),
            P(None, "grp"),
            P(None, "grp"),
            P("grp", None),
            P("blk", None),
            P("blk"),
        ),
        out_specs=P(("blk", "grp"), None),
        check_vma=False,
    )
```

```python
import functools
import math

import jax
import jax.numpy as jnp
from jax import lax
from jax.experimental import pallas as pl
from jax.experimental.pallas import tpu as pltpu
from jax.sharding import PartitionSpec as P

HEAD_WIDTH = 128
MASK_BLOCK_TOKENS = 128
ROPE_BASE = 500000.0
NEG_FILL = -1e30
QUERY_COLS = 1024
WIDE = 8
MOST = 7
SURE = 6
QUERY_FACTOR = HEAD_WIDTH**-0.5 * math.log2(math.e)
ANY = pl.BlockSpec(memory_space=pl.ANY)
VMEM = pl.BlockSpec(memory_space=pltpu.VMEM)
SMEM = pl.BlockSpec(memory_space=pltpu.SMEM)
MIB = 1 << 20


def params(mib):
    return pltpu.CompilerParams(vmem_limit_bytes=mib * MIB)


def turn(product, cosine, sine):
    return product * cosine + pltpu.roll(product, HEAD_WIDTH // 2, 1) * sine


def preload_kernel(count, *refs):
    sources, targets, sems = refs[:count], refs[-1 - count : -1], refs[-1]
    copies = [
        pltpu.make_async_copy(source, target, sems.at[at])
        for at, (source, target) in enumerate(zip(sources, targets))
    ]
    for copy in copies:
        copy.start()
    for copy in copies:
        copy.wait()


def preload(weights, after):
    return pl.pallas_call(
        functools.partial(preload_kernel, len(weights)),
        out_shape=[pltpu.VMEM(weight.shape, weight.dtype) for weight in weights],
        in_specs=[ANY] * (len(weights) + len(after)),
        out_specs=[VMEM] * len(weights),
        scratch_shapes=[pltpu.SemaphoreType.DMA((len(weights),))],
        compiler_params=params(1),
        name="preload",
    )(*[pltpu.with_memory_space_constraint(weight, pltpu.HBM) for weight in weights], *after)


def kept(weight):
    return pltpu.with_memory_space_constraint(weight, pltpu.VMEM)


def group_of(slot, core):
    return {0: 0, 1: 1 + core, 2: 2 - core, 3: 3}[slot]


def chip_of(at, chips):
    shift, step, place = 0, chips // 2, 1
    while step:
        shift = shift ^ ((at // place % 2) * (2 * step - 1))
        step, place = step // 2, place * 2
    return shift


def table_rows(ref, slots, piece_rows):
    if slots is None:
        return ref[...]
    grp, core = lax.axis_index("grp"), lax.axis_index("blk") % 2
    rows = []
    for slot in slots:
        at = lax.bitwise_xor(grp, group_of(slot, core)) * piece_rows
        rows.append(ref[pl.ds(pl.multiple_of(at, piece_rows), piece_rows)])
    return jnp.concatenate(rows, axis=0)


def key_value_kernel(count, slots, *refs):
    pieces, (key_ref, value_ref, cos_ref, sin_ref, *_, out_ref) = refs[:count], refs[count:]
    width = key_ref.shape[1]
    rows = jnp.concatenate([piece[...] for piece in pieces], axis=0)
    keys = jnp.dot(rows, key_ref[...], preferred_element_type=jnp.float32)
    values = jnp.dot(rows, value_ref[...], preferred_element_type=jnp.float32)
    cosine = table_rows(cos_ref, slots, pieces[0].shape[0])
    sine = table_rows(sin_ref, slots, pieces[0].shape[0])
    for at in range(0, width, HEAD_WIDTH):
        head = slice(at, at + HEAD_WIDTH)
        out_ref[:, head] = turn(keys[:, head], cosine, sine).astype(out_ref.dtype)
    out_ref[:, width:] = values.astype(out_ref.dtype)


def key_value_rows(
    pieces, key_weight, value_weight, cosine, sine, slots=None, after=(), weigh=1
):
    rows = sum(piece.shape[0] for piece in pieces)
    width = key_weight.shape[1] + value_weight.shape[1]
    return pl.pallas_call(
        functools.partial(key_value_kernel, len(pieces), slots),
        out_shape=jax.ShapeDtypeStruct((rows, width), jnp.bfloat16),
        in_specs=[VMEM] * (len(pieces) + 4) + [ANY] * len(after),
        out_specs=VMEM,
        compiler_params=params(16),
        cost_estimate=pl.CostEstimate(
            flops=2 * rows * (key_weight.size + value_weight.size) * weigh,
            bytes_accessed=2 * (key_weight.size + value_weight.size),
            transcendentals=0,
        ),
        name="key_value_rows",
    )(*pieces, key_weight, value_weight, cosine, sine, *after)


def query_kernel(slots, *refs):
    count = len(refs) - 4
    pieces, (weight_ref, cos_ref, sin_ref, out_ref) = refs[:count], refs[count:]
    rows = jnp.concatenate([piece[...] for piece in pieces], axis=0)
    cosine = table_rows(cos_ref, slots, pieces[0].shape[0]) * QUERY_FACTOR
    sine = table_rows(sin_ref, slots, pieces[0].shape[0]) * QUERY_FACTOR
    step = min(weight_ref.shape[1], QUERY_COLS)

    @pl.loop(0, weight_ref.shape[1] // step)
    def _(tile):
        at = pl.multiple_of(tile * step, step)
        product = jnp.dot(rows, weight_ref[:, pl.ds(at, step)], preferred_element_type=jnp.float32)
        for head in range(0, step, HEAD_WIDTH):
            turned = turn(product[:, head : head + HEAD_WIDTH], cosine, sine)
            out_ref[:, pl.ds(at + head, HEAD_WIDTH)] = turned.astype(out_ref.dtype)


def query_rows(pieces, weight, cosine, sine, slots=None):
    rows = sum(piece.shape[0] for piece in pieces)
    return pl.pallas_call(
        functools.partial(query_kernel, slots),
        out_shape=jax.ShapeDtypeStruct((rows, weight.shape[1]), jnp.bfloat16),
        in_specs=[VMEM] * (len(pieces) + 3),
        out_specs=VMEM,
        compiler_params=params(18),
        cost_estimate=pl.CostEstimate(
            flops=2 * rows * weight.size, bytes_accessed=2 * weight.size, transcendentals=0
        ),
        name="query_rows",
    )(*pieces, weight, cosine, sine)


def attend_kernel(slots, held, placed, mask_ref, query_ref, kv_ref, weight_ref, *rest):
    out_refs, (live_ref, mixed_ref) = rest[: len(slots)], rest[len(slots) :]
    grp, core = lax.axis_index("grp"), lax.axis_index("blk") % 2
    piece_rows = query_ref.shape[0] // len(held)
    kv_heads = kv_ref.shape[1] // (2 * HEAD_WIDTH)
    repeat = query_ref.shape[1] // (kv_heads * HEAD_WIDTH)
    block = MASK_BLOCK_TOKENS

    for at, slot in enumerate(slots):
        query_piece = lax.bitwise_xor(grp, group_of(slot, core)) if placed else slot
        query_block = query_piece * piece_rows // block

        def note(index, count, query_block=query_block):
            live_ref[count] = index
            return count + mask_ref[query_block, index]

        count = lax.fori_loop(0, mask_ref.shape[1], note, jnp.int32(0), unroll=16)
        for spare in range(WIDE):
            live_ref[count + spare] = 0

        queries = [
            jnp.concatenate(
                [
                    query_ref[
                        held.index(slot) * piece_rows : (held.index(slot) + 1) * piece_rows,
                        (head * repeat + q) * HEAD_WIDTH : (head * repeat + q + 1) * HEAD_WIDTH,
                    ]
                    for q in range(repeat)
                ],
                axis=0,
            )
            for head in range(kv_heads)
        ]
        ones = jnp.ones((WIDE * block, HEAD_WIDTH), jnp.bfloat16)

        def step(index, state, queries=queries, count=count, width=WIDE):
            first = index * WIDE
            starts = [
                pl.multiple_of(live_ref[first + wide] * block, block) for wide in range(width)
            ]
            new_state = []
            for head, query in enumerate(queries):
                key_cols = slice(head * HEAD_WIDTH, (head + 1) * HEAD_WIDTH)
                value_cols = slice(
                    (kv_heads + head) * HEAD_WIDTH, (kv_heads + head + 1) * HEAD_WIDTH
                )
                keys = jnp.concatenate(
                    [kv_ref[pl.ds(start, block), key_cols] for start in starts], axis=0
                )
                values = jnp.concatenate(
                    [kv_ref[pl.ds(start, block), value_cols] for start in starts], axis=0
                )
                scores = lax.dot_general(
                    query, keys, (((1,), (1,)), ((), ())), preferred_element_type=jnp.float32
                )
                scores = jnp.concatenate(
                    [scores[:, : SURE * block]]
                    + [
                        scores[:, wide * block : (wide + 1) * block]
                        + jnp.where(first + wide < count, 0.0, NEG_FILL)
                        for wide in range(SURE, width)
                    ],
                    axis=1,
                )
                top = jnp.max(scores, axis=1, keepdims=True)
                if state is not None:
                    top = jnp.maximum(state[2 * head], top)
                weights = jnp.exp2(scores - top).astype(jnp.bfloat16)
                sums = jnp.dot(
                    weights,
                    jnp.concatenate([values, ones[: width * block]], axis=1),
                    preferred_element_type=jnp.float32,
                )
                if state is not None:
                    sums = sums + state[2 * head + 1] * jnp.exp2(state[2 * head] - top)
                new_state += [top, sums]
            return tuple(new_state)

        def many_steps(step=step, count=count):
            one, two = step(0, None), step(1, None)
            state = []
            for head in range(kv_heads):
                top = jnp.maximum(one[2 * head], two[2 * head])
                state += [
                    top,
                    one[2 * head + 1] * jnp.exp2(one[2 * head] - top)
                    + two[2 * head + 1] * jnp.exp2(two[2 * head] - top),
                ]
            return lax.fori_loop(2, (count + WIDE - 1) // WIDE, step, tuple(state))

        state = lax.cond(count > MOST, many_steps, functools.partial(step, 0, None, width=MOST))
        for head in range(kv_heads):
            sums = state[2 * head + 1]
            mixed = (sums[:, :HEAD_WIDTH] / sums[:, HEAD_WIDTH:]).astype(jnp.bfloat16)
            for q in range(repeat):
                mixed_ref[
                    at * piece_rows : (at + 1) * piece_rows,
                    (head * repeat + q) * HEAD_WIDTH : (head * repeat + q + 1) * HEAD_WIDTH,
                ] = mixed[q * piece_rows : (q + 1) * piece_rows]

    tile_cols = weight_ref.shape[1] if mixed_ref.shape[0] <= 128 else 512

    @pl.loop(0, weight_ref.shape[1] // tile_cols)
    def _(tile):
        here = pl.ds(pl.multiple_of(tile * tile_cols, tile_cols), tile_cols)
        term = jnp.dot(
            mixed_ref[...], weight_ref[:, here], preferred_element_type=jnp.float32
        ).astype(jnp.bfloat16)
        for at in range(len(slots)):
            out_refs[at][:, here] = term[at * piece_rows : (at + 1) * piece_rows]


def gather_kernel(chunks, *refs):
    parts, out_ref = refs[:-1], refs[-1]
    grp, blk = lax.axis_index("grp"), lax.axis_index("blk")

    def place(owner, group, rows):
        at = (owner * 4 + group) * rows.shape[0]
        out_ref[pl.ds(pl.multiple_of(at, rows.shape[0]), rows.shape[0])] = rows

    at = 0
    for slots in chunks:
        shifts = parts[at].shape[0]
        piece_rows = parts[at].shape[1] // len(slots)
        for other in range(2):
            core = lax.bitwise_xor(blk % 2, other)
            for shift in range(shifts):
                owner = lax.bitwise_xor(blk // 2, chip_of(shift, shifts)) * 2 + core
                for index, slot in enumerate(slots):
                    group = lax.bitwise_xor(grp, group_of(slot, core))
                    rows = slice(index * piece_rows, (index + 1) * piece_rows)
                    place(owner, group, parts[at + other][shift, rows])
        at += 2


def gather_rows(chunks, parts, rows):
    return pl.pallas_call(
        functools.partial(gather_kernel, chunks),
        out_shape=jax.ShapeDtypeStruct((rows, parts[0].shape[-1]), jnp.bfloat16),
        in_specs=[VMEM] * len(parts),
        out_specs=VMEM,
        compiler_params=params(12),
        name="key_value_gather",
    )(*parts)


def attend(slots, held, placed, mask, query, kv, weight):
    piece_rows = query.shape[0] // len(held)
    term = jax.ShapeDtypeStruct((piece_rows, weight.shape[1]), jnp.bfloat16)
    return pl.pallas_call(
        functools.partial(attend_kernel, slots, held, placed),
        out_shape=[term] * len(slots),
        in_specs=[SMEM, VMEM, VMEM, VMEM],
        out_specs=[VMEM] * len(slots),
        scratch_shapes=[
            pltpu.SMEM((mask.shape[1] + 2 * WIDE,), jnp.int32),
            pltpu.VMEM((len(slots) * piece_rows, weight.shape[0]), jnp.bfloat16),
        ],
        compiler_params=params(20 if placed else 48),
        cost_estimate=pl.CostEstimate(
            flops=2 * len(slots) * piece_rows * weight.size * 2,
            bytes_accessed=2 * weight.size,
            transcendentals=0,
        ),
        name="attend_project",
    )(mask, query, kv, weight)


def rotary_tables(positions):
    half = HEAD_WIDTH // 2
    inverse = jnp.power(
        jnp.float32(ROPE_BASE),
        -(2.0 * (jnp.arange(HEAD_WIDTH) % half).astype(jnp.float32)) / HEAD_WIDTH,
    )
    sign = jnp.where(jnp.arange(HEAD_WIDTH) < half, -1.0, 1.0)
    angles = positions.astype(jnp.float32)[:, None] * inverse[None, :]
    return jnp.cos(angles), jnp.sin(angles) * sign[None, :]


def add(*values):
    total = values[0].astype(jnp.float32)
    for value in values[1:]:
        total = total + value.astype(jnp.float32)
    return total.astype(jnp.bfloat16)


def general_body(
    blk_count, groups, tokens, w_query, key_weight, value_weight, w_output, block_mask, positions
):
    rows = lax.all_gather(tokens, "grp", axis=0, tiled=True)
    cosine, sine = rotary_tables(positions)
    own = key_value_rows((rows,), key_weight, value_weight, cosine, sine)
    kv = lax.all_gather(own, "blk", axis=0, tiled=True)
    query = query_rows((rows,), w_query, cosine, sine)
    order = tuple(range(groups))
    terms = attend(order, order, False, block_mask, query, kv, w_output)
    term = jnp.concatenate(terms, axis=0)
    return lax.psum_scatter(term, "grp", scatter_dimension=0, tiled=True)


def square_body(
    blk_count, tokens, w_query, key_weight, value_weight, w_output, block_mask, positions
):
    chips = blk_count // 2

    def send(value, slot):
        pairs = []
        for g in range(4):
            for b in range(blk_count):
                pairs.append((g * blk_count + b, (g ^ group_of(slot, b % 2)) * blk_count + b))
        return lax.ppermute(value, ("grp", "blk"), pairs)

    first, second = send(tokens, 1), send(tokens, 2)
    across = send(first, 2)

    cosine, sine = rotary_tables(positions)
    key_weight, value_weight = preload((key_weight, value_weight), (cosine, sine))

    def exchange(slots, after=(), direct=True):
        own = key_value_rows(
            [pieces[slot] for slot in slots],
            kept(key_weight),
            kept(value_weight),
            cosine,
            sine,
            slots,
            after,
        )
        def across_chips(value, by):
            return lax.ppermute(value, "blk", [(b, b ^ (2 * by)) for b in range(blk_count)])

        near, far = across_chips(own, 1), across_chips(own, 3)
        if direct:
            last = across_chips(own, 2)
        else:
            near, far = lax.optimization_barrier((near, far))
            last = across_chips(far, 1)
        held = jnp.stack([own, far, near, last])
        return own, held

    def with_other_core(*held):
        held = jnp.concatenate(held, axis=1)
        return [held, lax.ppermute(held, "blk", [(b, b ^ 1) for b in range(blk_count)])]

    pieces = (tokens, first, second, across)
    rows_0, held_0 = exchange((0,), (), True)
    parts_0 = with_other_core(held_0)
    rows_1, held_1 = exchange((1, 2), parts_0, False)
    query_1 = query_rows(pieces[:3], w_query, cosine, sine, (0, 1, 2))
    rows_2, held_2 = exchange((3,), (rows_1, query_1), True)
    query_2 = query_rows(pieces[3:], w_query, cosine, sine, (3,))
    held_2, query_2 = lax.optimization_barrier((held_2, query_2))
    query = {(0, 1, 2): query_1, (3,): query_2}
    parts = parts_0 + with_other_core(held_1, held_2)
    chunks = ((0,), (1, 2, 3))
    kv = gather_rows(chunks, parts, blk_count * positions.shape[0])

    def terms(slots):
        held = next(held for held in query if slots[0] in held)
        return attend(slots, held, True, block_mask, query[held], kv, w_output)

    (term_across,) = terms((3,))
    sent_across = send(term_across, 2)
    (term_second,) = terms((2,))
    sent_second = send(term_second, 2)
    (term_first,) = terms((1,))
    sent_first = send(add(term_first, sent_across), 1)
    (term_own,) = terms((0,))
    return add(term_own, sent_second, sent_first)


def solution(mesh):
    groups, blk_count = mesh.shape["grp"], mesh.shape["blk"]
    if groups == 4 and blk_count == 8:
        body = functools.partial(square_body, blk_count)
    else:
        body = functools.partial(general_body, blk_count, groups)
    return jax.shard_map(
        body,
        mesh=mesh,
        in_specs=(
            P(("blk", "grp"), None),
            P(None, "grp"),
            P(None, "grp"),
            P(None, "grp"),
            P("grp", None),
            P("blk", None),
            P("blk"),
        ),
        out_specs=P(("blk", "grp"), None),
        check_vma=False,
    )
```

```python
import functools
import math

import jax
import jax.numpy as jnp
from jax import lax
from jax.experimental import pallas as pl
from jax.experimental.pallas import tpu as pltpu
from jax.sharding import PartitionSpec as P

HEAD_WIDTH = 128
MASK_BLOCK_TOKENS = 128
ROPE_BASE = 500000.0
NEG_FILL = -1e30
QUERY_COLS = 1024
WIDE = 8
MOST = 7
SURE = 6
QUERY_FACTOR = HEAD_WIDTH**-0.5 * math.log2(math.e)
ANY = pl.BlockSpec(memory_space=pl.ANY)
VMEM = pl.BlockSpec(memory_space=pltpu.VMEM)
SMEM = pl.BlockSpec(memory_space=pltpu.SMEM)
MIB = 1 << 20


def params(mib):
    return pltpu.CompilerParams(vmem_limit_bytes=mib * MIB)


def turn(product, cosine, sine):
    return product * cosine + pltpu.roll(product, HEAD_WIDTH // 2, 1) * sine


def preload_kernel(count, *refs):
    sources, targets, sems = refs[:count], refs[-1 - count : -1], refs[-1]
    copies = [
        pltpu.make_async_copy(source, target, sems.at[at])
        for at, (source, target) in enumerate(zip(sources, targets))
    ]
    for copy in copies:
        copy.start()
    for copy in copies:
        copy.wait()


def preload(weights, after):
    return pl.pallas_call(
        functools.partial(preload_kernel, len(weights)),
        out_shape=[pltpu.VMEM(weight.shape, weight.dtype) for weight in weights],
        in_specs=[ANY] * (len(weights) + len(after)),
        out_specs=[VMEM] * len(weights),
        scratch_shapes=[pltpu.SemaphoreType.DMA((len(weights),))],
        compiler_params=params(1),
        name="preload",
    )(*[pltpu.with_memory_space_constraint(weight, pltpu.HBM) for weight in weights], *after)


def kept(weight):
    return pltpu.with_memory_space_constraint(weight, pltpu.VMEM)


def group_of(slot, core):
    return {0: 0, 1: 1 + core, 2: 2 - core, 3: 3}[slot]


def chip_of(at, chips):
    shift, step, place = 0, chips // 2, 1
    while step:
        shift = shift ^ ((at // place % 2) * (2 * step - 1))
        step, place = step // 2, place * 2
    return shift


def table_rows(ref, slots, piece_rows):
    if slots is None:
        return ref[...]
    grp, core = lax.axis_index("grp"), lax.axis_index("blk") % 2
    rows = []
    for slot in slots:
        at = lax.bitwise_xor(grp, group_of(slot, core)) * piece_rows
        rows.append(ref[pl.ds(pl.multiple_of(at, piece_rows), piece_rows)])
    return jnp.concatenate(rows, axis=0)


def key_value_kernel(count, slots, *refs):
    pieces, (key_ref, value_ref, cos_ref, sin_ref, *_, out_ref) = refs[:count], refs[count:]
    width = key_ref.shape[1]
    rows = jnp.concatenate([piece[...] for piece in pieces], axis=0)
    keys = jnp.dot(rows, key_ref[...], preferred_element_type=jnp.float32)
    values = jnp.dot(rows, value_ref[...], preferred_element_type=jnp.float32)
    cosine = table_rows(cos_ref, slots, pieces[0].shape[0])
    sine = table_rows(sin_ref, slots, pieces[0].shape[0])
    for at in range(0, width, HEAD_WIDTH):
        head = slice(at, at + HEAD_WIDTH)
        out_ref[:, head] = turn(keys[:, head], cosine, sine).astype(out_ref.dtype)
    out_ref[:, width:] = values.astype(out_ref.dtype)


def key_value_rows(
    pieces, key_weight, value_weight, cosine, sine, slots=None, after=(), weigh=1
):
    rows = sum(piece.shape[0] for piece in pieces)
    width = key_weight.shape[1] + value_weight.shape[1]
    return pl.pallas_call(
        functools.partial(key_value_kernel, len(pieces), slots),
        out_shape=jax.ShapeDtypeStruct((rows, width), jnp.bfloat16),
        in_specs=[VMEM] * (len(pieces) + 4) + [ANY] * len(after),
        out_specs=VMEM,
        compiler_params=params(16),
        cost_estimate=pl.CostEstimate(
            flops=2 * rows * (key_weight.size + value_weight.size) * weigh,
            bytes_accessed=2 * (key_weight.size + value_weight.size),
            transcendentals=0,
        ),
        name="key_value_rows",
    )(*pieces, key_weight, value_weight, cosine, sine, *after)


def query_kernel(slots, *refs):
    count = len(refs) - 4
    pieces, (weight_ref, cos_ref, sin_ref, out_ref) = refs[:count], refs[count:]
    rows = jnp.concatenate([piece[...] for piece in pieces], axis=0)
    cosine = table_rows(cos_ref, slots, pieces[0].shape[0]) * QUERY_FACTOR
    sine = table_rows(sin_ref, slots, pieces[0].shape[0]) * QUERY_FACTOR
    step = min(weight_ref.shape[1], QUERY_COLS)

    @pl.loop(0, weight_ref.shape[1] // step)
    def _(tile):
        at = pl.multiple_of(tile * step, step)
        product = jnp.dot(rows, weight_ref[:, pl.ds(at, step)], preferred_element_type=jnp.float32)
        for head in range(0, step, HEAD_WIDTH):
            turned = turn(product[:, head : head + HEAD_WIDTH], cosine, sine)
            out_ref[:, pl.ds(at + head, HEAD_WIDTH)] = turned.astype(out_ref.dtype)


def query_rows(pieces, weight, cosine, sine, slots=None):
    rows = sum(piece.shape[0] for piece in pieces)
    return pl.pallas_call(
        functools.partial(query_kernel, slots),
        out_shape=jax.ShapeDtypeStruct((rows, weight.shape[1]), jnp.bfloat16),
        in_specs=[VMEM] * (len(pieces) + 3),
        out_specs=VMEM,
        compiler_params=params(18),
        cost_estimate=pl.CostEstimate(
            flops=2 * rows * weight.size, bytes_accessed=2 * weight.size, transcendentals=0
        ),
        name="query_rows",
    )(*pieces, weight, cosine, sine)


def attend_kernel(slots, held, placed, mask_ref, query_ref, kv_ref, weight_ref, *rest):
    out_refs, (live_ref, mixed_ref) = rest[: len(slots)], rest[len(slots) :]
    grp, core = lax.axis_index("grp"), lax.axis_index("blk") % 2
    piece_rows = query_ref.shape[0] // len(held)
    kv_heads = kv_ref.shape[1] // (2 * HEAD_WIDTH)
    repeat = query_ref.shape[1] // (kv_heads * HEAD_WIDTH)
    block = MASK_BLOCK_TOKENS

    for at, slot in enumerate(slots):
        query_piece = lax.bitwise_xor(grp, group_of(slot, core)) if placed else slot
        query_block = query_piece * piece_rows // block

        def note(index, count, query_block=query_block):
            live_ref[count] = index
            return count + mask_ref[query_block, index]

        count = lax.fori_loop(0, mask_ref.shape[1], note, jnp.int32(0), unroll=16)
        for spare in range(WIDE):
            live_ref[count + spare] = 0

        queries = [
            jnp.concatenate(
                [
                    query_ref[
                        held.index(slot) * piece_rows : (held.index(slot) + 1) * piece_rows,
                        (head * repeat + q) * HEAD_WIDTH : (head * repeat + q + 1) * HEAD_WIDTH,
                    ]
                    for q in range(repeat)
                ],
                axis=0,
            )
            for head in range(kv_heads)
        ]
        ones = jnp.ones((2 * WIDE * block, HEAD_WIDTH), jnp.bfloat16)

        def step(index, state, queries=queries, count=count, width=WIDE):
            first = index * WIDE
            starts = [
                pl.multiple_of(live_ref[first + wide] * block, block) for wide in range(width)
            ]
            new_state = []
            for head, query in enumerate(queries):
                key_cols = slice(head * HEAD_WIDTH, (head + 1) * HEAD_WIDTH)
                value_cols = slice(
                    (kv_heads + head) * HEAD_WIDTH, (kv_heads + head + 1) * HEAD_WIDTH
                )
                keys = jnp.concatenate(
                    [kv_ref[pl.ds(start, block), key_cols] for start in starts], axis=0
                )
                values = jnp.concatenate(
                    [kv_ref[pl.ds(start, block), value_cols] for start in starts], axis=0
                )
                scores = lax.dot_general(
                    query, keys, (((1,), (1,)), ((), ())), preferred_element_type=jnp.float32
                )
                scores = jnp.concatenate(
                    [scores[:, : SURE * block]]
                    + [
                        scores[:, wide * block : (wide + 1) * block]
                        + jnp.where(first + wide < count, 0.0, NEG_FILL)
                        for wide in range(SURE, width)
                    ],
                    axis=1,
                )
                top = jnp.max(scores, axis=1, keepdims=True)
                if state is not None:
                    top = jnp.maximum(state[2 * head], top)
                weights = jnp.exp2(scores - top).astype(jnp.bfloat16)
                sums = jnp.dot(
                    weights,
                    jnp.concatenate([values, ones[: width * block]], axis=1),
                    preferred_element_type=jnp.float32,
                )
                if state is not None:
                    sums = sums + state[2 * head + 1] * jnp.exp2(state[2 * head] - top)
                new_state += [top, sums]
            return tuple(new_state)

        def many_steps(step=step, count=count):
            state = step(0, None, width=2 * WIDE)
            return lax.fori_loop(2, (count + WIDE - 1) // WIDE, step, state)

        state = lax.cond(count > MOST, many_steps, functools.partial(step, 0, None, width=MOST))
        for head in range(kv_heads):
            sums = state[2 * head + 1]
            mixed = (sums[:, :HEAD_WIDTH] / sums[:, HEAD_WIDTH:]).astype(jnp.bfloat16)
            for q in range(repeat):
                mixed_ref[
                    at * piece_rows : (at + 1) * piece_rows,
                    (head * repeat + q) * HEAD_WIDTH : (head * repeat + q + 1) * HEAD_WIDTH,
                ] = mixed[q * piece_rows : (q + 1) * piece_rows]

    tile_cols = weight_ref.shape[1] if mixed_ref.shape[0] <= 128 else 512

    @pl.loop(0, weight_ref.shape[1] // tile_cols)
    def _(tile):
        here = pl.ds(pl.multiple_of(tile * tile_cols, tile_cols), tile_cols)
        term = jnp.dot(
            mixed_ref[...], weight_ref[:, here], preferred_element_type=jnp.float32
        ).astype(jnp.bfloat16)
        for at in range(len(slots)):
            out_refs[at][:, here] = term[at * piece_rows : (at + 1) * piece_rows]


def gather_kernel(chunks, *refs):
    parts, out_ref = refs[:-1], refs[-1]
    grp, blk = lax.axis_index("grp"), lax.axis_index("blk")

    def place(owner, group, rows):
        at = (owner * 4 + group) * rows.shape[0]
        out_ref[pl.ds(pl.multiple_of(at, rows.shape[0]), rows.shape[0])] = rows

    at = 0
    for slots in chunks:
        shifts = parts[at].shape[0]
        piece_rows = parts[at].shape[1] // len(slots)
        for other in range(2):
            core = lax.bitwise_xor(blk % 2, other)
            for shift in range(shifts):
                owner = lax.bitwise_xor(blk // 2, chip_of(shift, shifts)) * 2 + core
                for index, slot in enumerate(slots):
                    group = lax.bitwise_xor(grp, group_of(slot, core))
                    rows = slice(index * piece_rows, (index + 1) * piece_rows)
                    place(owner, group, parts[at + other][shift, rows])
        at += 2


def gather_rows(chunks, parts, rows):
    return pl.pallas_call(
        functools.partial(gather_kernel, chunks),
        out_shape=jax.ShapeDtypeStruct((rows, parts[0].shape[-1]), jnp.bfloat16),
        in_specs=[VMEM] * len(parts),
        out_specs=VMEM,
        compiler_params=params(12),
        name="key_value_gather",
    )(*parts)


def attend(slots, held, placed, mask, query, kv, weight):
    piece_rows = query.shape[0] // len(held)
    term = jax.ShapeDtypeStruct((piece_rows, weight.shape[1]), jnp.bfloat16)
    return pl.pallas_call(
        functools.partial(attend_kernel, slots, held, placed),
        out_shape=[term] * len(slots),
        in_specs=[SMEM, VMEM, VMEM, VMEM],
        out_specs=[VMEM] * len(slots),
        scratch_shapes=[
            pltpu.SMEM((mask.shape[1] + 2 * WIDE,), jnp.int32),
            pltpu.VMEM((len(slots) * piece_rows, weight.shape[0]), jnp.bfloat16),
        ],
        compiler_params=params(20 if placed else 48),
        cost_estimate=pl.CostEstimate(
            flops=2 * len(slots) * piece_rows * weight.size * 2,
            bytes_accessed=2 * weight.size,
            transcendentals=0,
        ),
        name="attend_project",
    )(mask, query, kv, weight)


def rotary_tables(positions):
    half = HEAD_WIDTH // 2
    inverse = jnp.power(
        jnp.float32(ROPE_BASE),
        -(2.0 * (jnp.arange(HEAD_WIDTH) % half).astype(jnp.float32)) / HEAD_WIDTH,
    )
    sign = jnp.where(jnp.arange(HEAD_WIDTH) < half, -1.0, 1.0)
    angles = positions.astype(jnp.float32)[:, None] * inverse[None, :]
    return jnp.cos(angles), jnp.sin(angles) * sign[None, :]


def add(*values):
    total = values[0].astype(jnp.float32)
    for value in values[1:]:
        total = total + value.astype(jnp.float32)
    return total.astype(jnp.bfloat16)


def general_body(
    blk_count, groups, tokens, w_query, key_weight, value_weight, w_output, block_mask, positions
):
    rows = lax.all_gather(tokens, "grp", axis=0, tiled=True)
    cosine, sine = rotary_tables(positions)
    own = key_value_rows((rows,), key_weight, value_weight, cosine, sine)
    kv = lax.all_gather(own, "blk", axis=0, tiled=True)
    query = query_rows((rows,), w_query, cosine, sine)
    order = tuple(range(groups))
    terms = attend(order, order, False, block_mask, query, kv, w_output)
    term = jnp.concatenate(terms, axis=0)
    return lax.psum_scatter(term, "grp", scatter_dimension=0, tiled=True)


def square_body(
    blk_count, tokens, w_query, key_weight, value_weight, w_output, block_mask, positions
):
    chips = blk_count // 2

    def send(value, slot):
        pairs = []
        for g in range(4):
            for b in range(blk_count):
                pairs.append((g * blk_count + b, (g ^ group_of(slot, b % 2)) * blk_count + b))
        return lax.ppermute(value, ("grp", "blk"), pairs)

    first, second = send(tokens, 1), send(tokens, 2)
    across = send(first, 2)

    cosine, sine = rotary_tables(positions)
    key_weight, value_weight = preload((key_weight, value_weight), (cosine, sine))

    def exchange(slots, after=(), direct=True):
        own = key_value_rows(
            [pieces[slot] for slot in slots],
            kept(key_weight),
            kept(value_weight),
            cosine,
            sine,
            slots,
            after,
        )
        def across_chips(value, by):
            return lax.ppermute(value, "blk", [(b, b ^ (2 * by)) for b in range(blk_count)])

        near, far = across_chips(own, 1), across_chips(own, 3)
        if direct:
            last = across_chips(own, 2)
        else:
            near, far = lax.optimization_barrier((near, far))
            last = across_chips(far, 1)
        held = jnp.stack([own, far, near, last])
        return own, held

    def with_other_core(*held):
        held = jnp.concatenate(held, axis=1)
        return [held, lax.ppermute(held, "blk", [(b, b ^ 1) for b in range(blk_count)])]

    pieces = (tokens, first, second, across)
    rows_0, held_0 = exchange((0,), (), True)
    parts_0 = with_other_core(held_0)
    rows_1, held_1 = exchange((1, 2), parts_0, False)
    query_1 = query_rows(pieces[:3], w_query, cosine, sine, (0, 1, 2))
    rows_2, held_2 = exchange((3,), (rows_1, query_1), True)
    query_2 = query_rows(pieces[3:], w_query, cosine, sine, (3,))
    held_2, query_2 = lax.optimization_barrier((held_2, query_2))
    query = {(0, 1, 2): query_1, (3,): query_2}
    parts = parts_0 + with_other_core(held_1, held_2)
    chunks = ((0,), (1, 2, 3))
    kv = gather_rows(chunks, parts, blk_count * positions.shape[0])

    def terms(slots):
        held = next(held for held in query if slots[0] in held)
        return attend(slots, held, True, block_mask, query[held], kv, w_output)

    (term_across,) = terms((3,))
    sent_across = send(term_across, 2)
    (term_second,) = terms((2,))
    sent_second = send(term_second, 2)
    (term_first,) = terms((1,))
    sent_first = send(add(term_first, sent_across), 1)
    (term_own,) = terms((0,))
    return add(term_own, sent_second, sent_first)


def solution(mesh):
    groups, blk_count = mesh.shape["grp"], mesh.shape["blk"]
    if groups == 4 and blk_count == 8:
        body = functools.partial(square_body, blk_count)
    else:
        body = functools.partial(general_body, blk_count, groups)
    return jax.shard_map(
        body,
        mesh=mesh,
        in_specs=(
            P(("blk", "grp"), None),
            P(None, "grp"),
            P(None, "grp"),
            P(None, "grp"),
            P("grp", None),
            P("blk", None),
            P("blk"),
        ),
        out_specs=P(("blk", "grp"), None),
        check_vma=False,
    )
```
